128 devices in a mesh: grp: 4 (over y_lo, core), dp: 32 (over x, y_hi, z).
Axes of the slice: x: 4, y: 4 (y_hi: 2, y_lo: 2; y = y_hi * 2 + y_lo), z: 4, core: 2. Of those that a mesh axis runs over, the one named last changes fastest.
Arguments:
- student: bfloat16 [64, 32, 32, 1280], P('dp', 'grp'), may hold values from -6 to 6
- dino_feat: bfloat16 [64, 36, 36, 1536], P('dp', None, None, 'grp'), may hold values from -6 to 6
- siglip_feat: bfloat16 [64, 36, 36, 1152], P('dp', None, None, 'grp'), may hold values from -6 to 6
- sam_feat: bfloat16 [64, 32, 32, 1280], P('dp', None, None, 'grp'), may hold values from -6 to 6
- w1_dino: bfloat16 [1280, 1536], replicated, may hold values from -0.15625 to 0.15625
- w2_dino: bfloat16 [1536, 1536], P(None, 'grp'), may hold values from -0.15625 to 0.15625
- w1_siglip: bfloat16 [1280, 1152], replicated, may hold values from -0.15625 to 0.15625
- w2_siglip: bfloat16 [1152, 1152], P(None, 'grp'), may hold values from -0.1875 to 0.1875
- w1_sam: bfloat16 [1280, 1280], replicated, may hold values from -0.15625 to 0.15625
- w2_sam: bfloat16 [1280, 1280], P(None, 'grp'), may hold values from -0.15625 to 0.15625
Outputs:
- grad_dino: float32 [1536, 1536], P('dp', 'grp')
- grad_siglip: float32 [1152, 1152], P('dp', 'grp')
- grad_sam: float32 [1280, 1280], P('dp', 'grp')
The draws below stay inside these ranges and needn't reach their ends.
All inputs are finite; a program needn't handle non-finite values.
Results may differ from the reference program's by a relative error of at most 0.012.
Values may be sent and summed in bfloat16 or wider, within the bound.
No kernel may reach another device: no remote copies, remote signals or barrier semaphores. Data moves between devices by JAX's collectives and lax.ppermute only.
A program may use at most 128 MiB of HBM per device.

```python
import math
import jax
import jax.numpy as jnp
from jax import lax

STUDENT_W = 1280
DINO_W = 1536
SIGLIP_W = 1152
SAM_W = 1280
GRID = 32
TGRID = 36
IMAGES = 64


def block_levels(own_key, dims, shards, smallest, largest):
    def one(axis_at, parts):
        steps = jax.random.uniform(jax.random.fold_in(jax.random.fold_in(own_key, 6), axis_at), (parts,), jnp.float32, smallest / len(shards), largest / len(shards))
        return jnp.repeat(jnp.exp(steps), dims[axis_at] // parts).reshape((-1,) + (1,) * (len(dims) - axis_at - 1))

    gain = one(*shards[0])
    for cut in shards[1:]:
        gain = gain * one(*cut)
    return gain


def centred(stream_key, extent, spread, limit, split=(), kind=jnp.bfloat16):
    array = spread * jax.random.normal(stream_key, extent, jnp.float32)
    if split:
        array = array * block_levels(stream_key, extent, split, -0.22, 0.18)
    return jnp.clip(array, -limit, limit).astype(kind)


def setup_inputs(seed: int = 0) -> dict:
    splits = jax.random.split(jax.random.key(seed), 11)
    return {
        "student": centred(splits[0], (IMAGES, GRID, GRID, STUDENT_W), 1.0, 6.0, ((0, 32), (1, 4))),
        "dino_feat": centred(splits[1], (IMAGES, TGRID, TGRID, DINO_W), 1.0, 6.0, ((0, 32), (3, 4))),
        "siglip_feat": centred(splits[2], (IMAGES, TGRID, TGRID, SIGLIP_W), 1.0, 6.0, ((0, 32), (3, 4))),
        "sam_feat": centred(splits[3], (IMAGES, GRID, GRID, SAM_W), 1.0, 6.0, ((0, 32), (3, 4))),
        "w1_dino": centred(splits[4], (STUDENT_W, DINO_W), STUDENT_W ** -0.5, 0.15625),
        "w2_dino": centred(splits[5], (DINO_W, DINO_W), DINO_W ** -0.5, 0.15625, ((1, 4),)),
        "w1_siglip": centred(splits[6], (STUDENT_W, SIGLIP_W), STUDENT_W ** -0.5, 0.15625),
        "w2_siglip": centred(splits[7], (SIGLIP_W, SIGLIP_W), SIGLIP_W ** -0.5, 0.1875, ((1, 4),)),
        "w1_sam": centred(splits[8], (STUDENT_W, SAM_W), STUDENT_W ** -0.5, 0.15625),
        "w2_sam": centred(splits[9], (SAM_W, SAM_W), SAM_W ** -0.5, 0.15625, ((1, 4),)),
    }


epsilon = 1e-06

def resample_matrix(fine, coarse):
    position = jnp.arange(fine, dtype=jnp.float32)
    source = jnp.clip((position + 0.5) * (coarse / fine) - 0.5, 0.0, coarse - 1.0)
    target = jnp.arange(coarse, dtype=jnp.float32)
    return jnp.maximum(0.0, 1.0 - jnp.abs(source[:, None] - target[None, :]))

def resampled(resample, feat):
    rows = jnp.einsum('st,ntuc->nsuc', resample, feat.astype(jnp.float32), precision=lax.Precision.HIGHEST)
    both = jnp.einsum('ut,nstc->nsuc', resample, rows, precision=lax.Precision.HIGHEST)
    return both.astype(jnp.bfloat16)

def adaptor_grad(tokens, target, w_first, w_second, scale):
    hidden = jax.nn.gelu(jnp.dot(tokens, w_first, preferred_element_type=jnp.float32)).astype(jnp.bfloat16)
    pred = jnp.dot(hidden, w_second, preferred_element_type=jnp.float32)
    goal = target.astype(jnp.float32)
    pred_norm = jnp.sqrt(lax.optimization_barrier(jnp.sum(pred * pred, axis=1, keepdims=True)) + epsilon)
    goal_norm = jnp.sqrt(lax.optimization_barrier(jnp.sum(goal * goal, axis=1, keepdims=True)) + epsilon)
    cosine = lax.optimization_barrier(jnp.sum(pred * goal, axis=1, keepdims=True)) / (pred_norm * goal_norm)
    error = (-scale * (goal / (pred_norm * goal_norm) - cosine * pred / (pred_norm * pred_norm))).astype(jnp.bfloat16)
    return jnp.einsum('tk,tc->kc', hidden, error, preferred_element_type=jnp.float32)

def reference(student, dino_feat, siglip_feat, sam_feat, w1_dino, w2_dino, w1_siglip, w2_siglip, w1_sam, w2_sam):
    images, grid, grid_cols, width = student.shape
    resample = resample_matrix(grid, dino_feat.shape[1])
    tokens = student.reshape(-1, width)
    total = images * grid * grid_cols
    outs = []
    for target, w_first, w_second in ((resampled(resample, dino_feat), w1_dino, w2_dino), (resampled(resample, siglip_feat), w1_siglip, w2_siglip), (sam_feat, w1_sam, w2_sam)):
        channels = target.shape[-1]
        scale = channels / math.sqrt(total)
        outs.append(adaptor_grad(tokens, target.reshape(-1, channels), w_first, w_second, scale))
    return (outs[0], outs[1], outs[2])
```

```python
import math

import jax
import jax.numpy as jnp
from jax import lax
from jax.sharding import PartitionSpec as P

epsilon = 1e-06

f32 = jnp.float32
bf16 = jnp.bfloat16

CORE = [(g, g ^ 1) for g in range(4)]
CHIP = [(g, g ^ 2) for g in range(4)]


def resample_matrix(fine, coarse):
    position = jnp.arange(fine, dtype=jnp.float32)
    source = jnp.clip((position + 0.5) * (coarse / fine) - 0.5, 0.0, coarse - 1.0)
    target = jnp.arange(coarse, dtype=jnp.float32)
    return jnp.maximum(0.0, 1.0 - jnp.abs(source[:, None] - target[None, :]))


def resampled(feat, grid, parts):
    n, coarse, _, width = feat.shape
    fine_run, coarse_run = grid // parts, coarse // parts
    cols = resample_matrix(grid, coarse)
    rows = cols[:fine_run, :coarse_run]
    both = (rows[:, None, :, None] * cols[None, :, None, :]).reshape(
        fine_run * grid, coarse_run * coarse
    )
    runs = feat.reshape(n, parts, coarse_run * coarse, width)
    return jnp.einsum(
        "sk,npkc->npsc", both.astype(bf16), runs, preferred_element_type=f32
    ).astype(bf16)


def shards(
    student,
    dino_feat,
    siglip_feat,
    sam_feat,
    w1_dino,
    w2_dino,
    w1_siglip,
    w2_siglip,
    w1_sam,
    w2_sam,
):
    n_images, row_count, grid, width = student.shape
    n_dp = lax.axis_size("dp")
    parts = lax.axis_size("grp")
    g = lax.axis_index("grp")
    total = n_images * n_dp * grid * grid
    own_tokens = n_images * row_count * grid

    own = student.reshape(own_tokens, width)
    pieces = 2
    step = own_tokens // pieces
    theirs = [
        lax.ppermute(own[i * step : (i + 1) * step], "grp", CHIP) for i in range(pieces)
    ]
    batches = [own] + theirs

    w1s = (w1_dino, w1_siglip, w1_sam)
    w2s = [
        jnp.concatenate([w, lax.ppermute(w, "grp", CORE)], axis=1)
        for w in (w2_dino, w2_siglip, w2_sam)
    ]

    run = row_count * grid
    grids = (
        resampled(dino_feat, grid, parts),
        resampled(siglip_feat, grid, parts),
        sam_feat.reshape(n_images, parts, run, sam_feat.shape[-1]),
    )

    def block(array, index):
        return lax.dynamic_index_in_dim(array, index, 1, keepdims=False).reshape(
            own_tokens, array.shape[-1]
        )

    goals = []
    for array in grids:
        mine = jnp.concatenate([block(array, g), block(array, g ^ 2)], axis=0)
        sent = jnp.concatenate([block(array, g ^ 1), block(array, g ^ 3)], axis=0)
        goals.append(jnp.concatenate([mine, lax.ppermute(sent, "grp", CORE)], axis=1))

    hiddens, preds, sums = [], [], []
    for goal, w_first, w_second in zip(goals, w1s, w2s):
        hidden = jnp.concatenate(
            [
                jax.nn.gelu(jnp.dot(b, w_first, preferred_element_type=f32)).astype(bf16)
                for b in batches
            ],
            axis=0,
        )
        pred = jnp.dot(hidden, w_second, preferred_element_type=f32)
        wide = goal.astype(f32)
        hiddens.append(hidden)
        preds.append(pred)
        sums.append(
            jnp.stack(
                [jnp.sum(pred * pred, 1), jnp.sum(wide * wide, 1), jnp.sum(pred * wide, 1)]
            )
        )

    outs = []
    for goal, hidden, pred, part in zip(goals, hiddens, preds, sums):
        channels = hidden.shape[1]
        scale = channels / math.sqrt(total)
        other = jnp.roll(lax.ppermute(part, "grp", CHIP), own_tokens, axis=1)
        pred_sq, goal_sq, cross = part + other
        pred_norm = jnp.sqrt(pred_sq + epsilon)[:, None]
        goal_norm = jnp.sqrt(goal_sq + epsilon)[:, None]
        cosine = cross[:, None] / (pred_norm * goal_norm)
        wide = goal.astype(f32)
        error = (
            -scale * (wide / (pred_norm * goal_norm) - cosine * pred / (pred_norm * pred_norm))
        ).astype(bf16)
        grad = jnp.einsum("tk,tc->kc", hidden, error, preferred_element_type=f32)
        local = grad.shape[1] // 2
        both = grad[:, :local] + lax.ppermute(grad[:, local:].astype(bf16), "grp", CORE).astype(f32)
        split = lax.all_to_all(
            both.astype(bf16).reshape(n_dp, channels // n_dp, local), "dp", 0, 0, tiled=True
        )
        outs.append(jnp.sum(split.astype(f32), axis=0))
    return (outs[0], outs[1], outs[2])


def solution(mesh):
    in_specs = (
        P("dp", "grp", None, None),
        P("dp", None, None, "grp"),
        P("dp", None, None, "grp"),
        P("dp", None, None, "grp"),
        P(),
        P(None, "grp"),
        P(),
        P(None, "grp"),
        P(),
        P(None, "grp"),
    )
    out_specs = (P("dp", "grp"), P("dp", "grp"), P("dp", "grp"))
    return jax.shard_map(shards, mesh=mesh, in_specs=in_specs, out_specs=out_specs, check_vma=False)
```

```python
import functools
import math

import jax
import jax.numpy as jnp
from jax import lax
from jax.experimental import pallas as pl
from jax.experimental.pallas import tpu as pltpu
from jax.sharding import PartitionSpec as P

epsilon = 1e-06

f32 = jnp.float32
bf16 = jnp.bfloat16

CORE = [(g, g ^ 1) for g in range(4)]
CHIP = [(g, g ^ 2) for g in range(4)]

HALF = 384
VMEM_LIMIT = 48 * 1024 * 1024


def pad_lanes(x):
    rows, width = x.shape
    if width == HALF:
        return x
    return jnp.concatenate([x, jnp.zeros((rows, HALF - width), x.dtype)], axis=1)


def resample_into(out_ref, feat_ref):
    _, in_rows, in_cols, width = feat_ref.shape
    out_rows = in_rows * 8 // 9
    slot = lax.broadcasted_iota(jnp.int32, (8, 1), 0).astype(f32)
    right = 0.125 * slot + 0.0625
    for r in range(out_rows):
        weight = 0.125 * (r % 8) + 0.0625
        first = r // 8 * 9 + r % 8
        row = (1.0 - weight) * feat_ref[0, first].astype(f32) + weight * feat_ref[
            0, first + 1
        ].astype(f32)
        blocks = []
        for b in range(in_cols // 9):
            blocks.append(
                (1.0 - right) * row[9 * b : 9 * b + 8] + right * row[9 * b + 1 : 9 * b + 9]
            )
        done = pad_lanes(jnp.concatenate(blocks, axis=0)).astype(bf16)
        count = done.shape[0]
        out_ref[0, 0, r * count : (r + 1) * count] = done


def targets_kernel(order_ref, dino, siglip, sam, dino_a, siglip_a, sam_a, dino_b, siglip_b, sam_b):
    def fill(dino_out, siglip_out, sam_out):
        resample_into(dino_out, dino)
        resample_into(siglip_out, siglip)
        _, rows, cols, width = sam.shape
        sam_out[0, 0] = pad_lanes(sam[0].reshape(rows * cols, width))

    slot = pl.program_id(0)

    @pl.when(slot < 2)
    def _():
        fill(dino_b, siglip_b, sam_b)

    @pl.when(slot >= 2)
    def _():
        fill(dino_a, siglip_a, sam_a)


def targets(order, dino, siglip, sam):
    n = sam.shape[0]
    run = sam.shape[1] // 4 * sam.shape[2]

    def block_of(feat):
        rows = feat.shape[1] // 4
        return pl.BlockSpec(
            (1, rows) + feat.shape[2:], lambda s, i, order: (i, order[s], 0, 0)
        )

    sent = pl.BlockSpec(
        (1, 1, run, HALF),
        lambda s, i, order: (jnp.minimum(s, 1), jnp.where(s < 2, i, n - 1), 0, 0),
    )
    kept = pl.BlockSpec(
        (1, 1, run, HALF),
        lambda s, i, order: (jnp.maximum(s, 2) - 2, jnp.where(s < 2, 0, i), 0, 0),
    )
    outs = pl.pallas_call(
        targets_kernel,
        grid_spec=pltpu.PrefetchScalarGridSpec(
            num_scalar_prefetch=1,
            grid=(4, n),
            in_specs=[block_of(dino), block_of(siglip), block_of(sam)],
            out_specs=[kept] * 3 + [sent] * 3,
        ),
        out_shape=[jax.ShapeDtypeStruct((2, n, run, HALF), bf16)] * 6,
        compiler_params=pltpu.CompilerParams(vmem_limit_bytes=VMEM_LIMIT),
        cost_estimate=pl.CostEstimate(flops=12_000_000, bytes_accessed=12_000_000, transcendentals=0),
        name="targets",
    )(order, dino, siglip, sam)
    flat = [o.reshape(2 * n * run, HALF) for o in outs]
    return flat[:3], flat[3:]


def gelu(x):
    inner = x * (0.7978845608028654 + (0.7978845608028654 * 0.044715) * (x * x))
    half = 0.5 * x
    return half + half * jnp.tanh(inner)


def adapt_kernel(steps, fresh, x, w1, w2o, w2s, goal_o, goal_s, *refs):
    hidden, pred, sums, w2 = refs if fresh else refs[3:]
    step = pl.program_id(0)
    width = w2o.shape[1]

    @pl.when(step == 0)
    def _():
        pred[...] = jnp.zeros_like(pred)
        if width < HALF:
            w2[...] = jnp.zeros_like(w2)

    w2[:, :width] = w2o[...]
    w2[:, HALF : HALF + width] = w2s[...]
    rows = x.shape[0]
    part = 256
    for m in range(rows // part):
        at = slice(m * part, (m + 1) * part)
        h = gelu(jnp.dot(x[at], w1[...], preferred_element_type=f32)).astype(bf16)
        hidden[at] = h
        pred[at] += jnp.dot(h, w2[...], preferred_element_type=f32)

    @pl.when(step == steps - 1)
    def _():
        for m in range(rows // part):
            at = slice(m * part, (m + 1) * part)
            p_o, p_s = pred[at, :HALF], pred[at, HALF:]
            t_o, t_s = goal_o[at].astype(f32), goal_s[at].astype(f32)

            def total(a, b):
                return jnp.sum(a + b, axis=1, keepdims=True)

            pred_sq = total(p_o * p_o, p_s * p_s)
            goal_sq = total(t_o * t_o, t_s * t_s)
            cross = total(p_o * t_o, p_s * t_s)
            lane = lax.broadcasted_iota(jnp.int32, (part, 128), 1)
            cols = jnp.where(lane == 0, pred_sq, jnp.where(lane == 1, goal_sq, cross))
            sums[:, at] = jnp.transpose(cols)[:8]


def adapt(x, which, w1, w2o, w2s, goal_o, goal_s, prior=None):
    rows, width = x.shape
    channels = w1.shape[1]
    tile = 512 if channels % 512 == 0 else (384 if channels % 384 == 0 else 256)
    steps = channels // tile
    anywhere = pl.BlockSpec(memory_space=pl.ANY)
    in_specs = [
        pl.BlockSpec((rows, width), lambda k: (0, 0)),
        pl.BlockSpec((width, tile), lambda k: (0, k)),
        pl.BlockSpec((tile, w2o.shape[1]), lambda k: (k, 0)),
        pl.BlockSpec((tile, w2o.shape[1]), lambda k: (k, 0)),
        pl.BlockSpec((rows, HALF), lambda k: (which, 0)),
        pl.BlockSpec((rows, HALF), lambda k: (which, 0)),
    ]
    args = (x, w1, w2o, w2s, goal_o, goal_s)
    aliases = {}
    if prior is not None:
        in_specs += [anywhere] * 3
        args += tuple(prior)
        aliases = {6: 0, 7: 1, 8: 2}
    return pl.pallas_call(
        functools.partial(adapt_kernel, steps, prior is None),
        grid=(steps,),
        in_specs=in_specs,
        out_specs=[
            pl.BlockSpec((rows, tile), lambda k: (which, k)),
            pl.BlockSpec((rows, 2 * HALF), lambda k: (which, 0)),
            pl.BlockSpec((8, rows), lambda k: (0, which)),
        ],
        out_shape=[
            jax.ShapeDtypeStruct((2 * rows, channels), bf16),
            jax.ShapeDtypeStruct((2 * rows, 2 * HALF), f32),
            jax.ShapeDtypeStruct((8, 2 * rows), f32),
        ],
        scratch_shapes=[pltpu.VMEM((tile, 2 * HALF), bf16)],
        input_output_aliases=aliases,
        compiler_params=pltpu.CompilerParams(vmem_limit_bytes=VMEM_LIMIT),
        cost_estimate=pl.CostEstimate(
            flops=2 * rows * channels * (width + 2 * HALF),
            bytes_accessed=2 * channels * (width + 2 * HALF + rows) + 4 * rows * 2 * HALF,
            transcendentals=rows * channels,
        ),
        name="adapt",
    )(*args)


def grad_kernel(scale, hidden, pred, goal_o, goal_s, sums, other, grad_o, grad_s, error):
    @pl.when(pl.program_id(0) == 0)
    def _():
        tokens = pred.shape[0]
        half = tokens // 2
        swapped = jnp.concatenate([other[:, half:], other[:, :half]], axis=1)
        both = sums[...] + swapped
        pred_norm = jnp.sqrt(both[0:1] + epsilon)
        goal_norm = jnp.sqrt(both[1:2] + epsilon)
        product = pred_norm * goal_norm
        cosine = both[2:3] / product
        on_goal = -scale / product
        on_pred = scale * cosine / (pred_norm * pred_norm)
        rows = lax.broadcasted_iota(jnp.int32, (128, tokens), 0)
        factors = jnp.transpose(jnp.where(rows == 0, on_goal, on_pred))
        part = 128
        for m in range(tokens // part):
            at = slice(m * part, (m + 1) * part)
            a, b = factors[at, 0:1], factors[at, 1:2]
            error[at, :HALF] = (a * goal_o[at].astype(f32) + b * pred[at, :HALF]).astype(bf16)
            error[at, HALF:] = (a * goal_s[at].astype(f32) + b * pred[at, HALF:]).astype(bf16)

    grad = lax.dot_general(
        hidden[...], error[...], (((0,), (0,)), ((), ())), preferred_element_type=f32
    )
    grad_o[...] = grad[:, :HALF]
    grad_s[...] = grad[:, HALF:].astype(bf16)


def gradient(scale, hidden, pred, goal_o, goal_s, sums, other):
    tokens, channels = hidden.shape
    tile = 384 if channels % 384 == 0 else 256
    whole = lambda shape: pl.BlockSpec(shape, lambda k: (0,) * len(shape))
    return pl.pallas_call(
        functools.partial(grad_kernel, scale),
        grid=(channels // tile,),
        in_specs=[
            pl.BlockSpec((tokens, tile), lambda k: (0, k)),
            whole(pred.shape),
            whole(goal_o.shape),
            whole(goal_s.shape),
            whole(sums.shape),
            whole(other.shape),
        ],
        out_specs=[pl.BlockSpec((tile, HALF), lambda k: (k, 0))] * 2,
        out_shape=[
            jax.ShapeDtypeStruct((channels, HALF), f32),
            jax.ShapeDtypeStruct((channels, HALF), bf16),
        ],
        scratch_shapes=[pltpu.VMEM((tokens, 2 * HALF), bf16)],
        compiler_params=pltpu.CompilerParams(vmem_limit_bytes=VMEM_LIMIT),
        cost_estimate=pl.CostEstimate(
            flops=2 * tokens * channels * 2 * HALF,
            bytes_accessed=2 * tokens * channels + 12 * tokens * HALF + 6 * channels * HALF,
            transcendentals=0,
        ),
        name="gradient",
    )(hidden, pred, goal_o, goal_s, sums, other)


def shards(
    student,
    dino_feat,
    siglip_feat,
    sam_feat,
    w1_dino,
    w2_dino,
    w1_siglip,
    w2_siglip,
    w1_sam,
    w2_sam,
):
    n_images, row_count, grid, width = student.shape
    n_dp = lax.axis_size("dp")
    g = lax.axis_index("grp")
    total = n_images * n_dp * grid * grid
    own_tokens = n_images * row_count * grid

    own = student.reshape(own_tokens, width)
    theirs = lax.ppermute(own, "grp", CHIP)

    w1s = (w1_dino, w1_sam, w1_siglip)
    w2s = (w2_dino, w2_sam, w2_siglip)
    w2_others = [lax.ppermute(w, "grp", CORE) for w in w2s]

    order = jnp.stack([g ^ 1, g ^ 3, g, g ^ 2]).astype(jnp.int32)
    kept, sent = targets(order, dino_feat, siglip_feat, sam_feat)
    kept = (kept[0], kept[2], kept[1])
    sent = (sent[0], sent[2], sent[1])
    goal_others = [lax.ppermute(s, "grp", CORE) for s in sent]

    firsts = [
        adapt(own, 0, w1, w2, w2x, goal, goalx)
        for w1, w2, w2x, goal, goalx in zip(w1s, w2s, w2_others, kept, goal_others)
    ]
    states = [
        adapt(theirs, 1, w1, w2, w2x, goal, goalx, prior=first)
        for w1, w2, w2x, goal, goalx, first in zip(
            w1s, w2s, w2_others, kept, goal_others, firsts
        )
    ]
    others = [lax.ppermute(s[2], "grp", CHIP) for s in states]

    locals_ = []
    for (hidden, pred, part), other, goal, goalx in zip(states, others, kept, goal_others):
        channels = hidden.shape[1]
        scale = channels / math.sqrt(total)
        grad_o, grad_s = gradient(scale, hidden, pred, goal, goalx, part, other)
        grad = grad_o + lax.ppermute(grad_s, "grp", CORE).astype(f32)
        locals_.append(grad.astype(bf16).reshape(n_dp, channels // n_dp, HALF))

    def over_images(parts):
        split = lax.all_to_all(parts, "dp", 0, 0, tiled=True)
        return jnp.sum(split.astype(f32), axis=0)

    dino = over_images(locals_[0])
    rest = over_images(jnp.concatenate(locals_[1:], axis=1))
    sam_rows = locals_[1].shape[1]
    return (
        dino[:, : w2_dino.shape[1]],
        rest[sam_rows:, : w2_siglip.shape[1]],
        rest[:sam_rows, : w2_sam.shape[1]],
    )


def solution(mesh):
    in_specs = (
        P("dp", "grp", None, None),
        P("dp", None, None, "grp"),
        P("dp", None, None, "grp"),
        P("dp", None, None, "grp"),
        P(),
        P(None, "grp"),
        P(),
        P(None, "grp"),
        P(),
        P(None, "grp"),
    )
    out_specs = (P("dp", "grp"), P("dp", "grp"), P("dp", "grp"))
    return jax.shard_map(shards, mesh=mesh, in_specs=in_specs, out_specs=out_specs, check_vma=False)
```

```python
import functools
import math

import jax
import jax.numpy as jnp
from jax import lax
from jax.experimental import pallas as pl
from jax.experimental.pallas import tpu as pltpu
from jax.sharding import PartitionSpec as P

epsilon = 1e-06

f32 = jnp.float32
bf16 = jnp.bfloat16

CORE = [(g, g ^ 1) for g in range(4)]
CHIP = [(g, g ^ 2) for g in range(4)]

HALF = 384
VMEM_LIMIT = 48 * 1024 * 1024


def pad_lanes(x):
    rows, width = x.shape
    if width == HALF:
        return x
    return jnp.concatenate([x, jnp.zeros((rows, HALF - width), x.dtype)], axis=1)


def resample_into(out_ref, feat_ref):
    _, in_rows, in_cols, width = feat_ref.shape
    out_rows = in_rows * 8 // 9
    slot = lax.broadcasted_iota(jnp.int32, (8, 1), 0).astype(f32)
    right = 0.125 * slot + 0.0625
    for r in range(out_rows):
        weight = 0.125 * (r % 8) + 0.0625
        first = r // 8 * 9 + r % 8
        row = (1.0 - weight) * feat_ref[0, first].astype(f32) + weight * feat_ref[
            0, first + 1
        ].astype(f32)
        blocks = []
        for b in range(in_cols // 9):
            blocks.append(
                (1.0 - right) * row[9 * b : 9 * b + 8] + right * row[9 * b + 1 : 9 * b + 9]
            )
        done = pad_lanes(jnp.concatenate(blocks, axis=0)).astype(bf16)
        count = done.shape[0]
        out_ref[0, 0, r * count : (r + 1) * count] = done


def targets_kernel(order_ref, dino, siglip, sam, dino_a, siglip_a, sam_a, dino_b, siglip_b, sam_b):
    def fill(dino_out, siglip_out, sam_out):
        resample_into(dino_out, dino)
        resample_into(siglip_out, siglip)
        _, rows, cols, width = sam.shape
        sam_out[0, 0] = pad_lanes(sam[0].reshape(rows * cols, width))

    slot = pl.program_id(0)

    @pl.when(slot < 2)
    def _():
        fill(dino_b, siglip_b, sam_b)

    @pl.when(slot >= 2)
    def _():
        fill(dino_a, siglip_a, sam_a)


def targets(order, dino, siglip, sam):
    n = sam.shape[0]
    run = sam.shape[1] // 4 * sam.shape[2]

    def block_of(feat):
        rows = feat.shape[1] // 4
        return pl.BlockSpec(
            (1, rows) + feat.shape[2:], lambda s, i, order: (i, order[s], 0, 0)
        )

    sent = pl.BlockSpec(
        (1, 1, run, HALF),
        lambda s, i, order: (jnp.minimum(s, 1), jnp.where(s < 2, i, n - 1), 0, 0),
    )
    kept = pl.BlockSpec(
        (1, 1, run, HALF),
        lambda s, i, order: (jnp.maximum(s, 2) - 2, jnp.where(s < 2, 0, i), 0, 0),
    )
    outs = pl.pallas_call(
        targets_kernel,
        grid_spec=pltpu.PrefetchScalarGridSpec(
            num_scalar_prefetch=1,
            grid=(4, n),
            in_specs=[block_of(dino), block_of(siglip), block_of(sam)],
            out_specs=[kept] * 3 + [sent] * 3,
        ),
        out_shape=[jax.ShapeDtypeStruct((2, n, run, HALF), bf16)] * 6,
        compiler_params=pltpu.CompilerParams(vmem_limit_bytes=VMEM_LIMIT),
        cost_estimate=pl.CostEstimate(flops=12_000_000, bytes_accessed=12_000_000, transcendentals=0),
        name="targets",
    )(order, dino, siglip, sam)
    flat = [o.reshape(2 * n * run, HALF) for o in outs]
    return flat[:3], flat[3:]


def gelu(x):
    inner = x * (0.7978845608028654 + (0.7978845608028654 * 0.044715) * (x * x))
    half = 0.5 * x
    return half + half * jnp.tanh(inner)


def copies_of(refs, n):
    return refs[:n], refs[n:]


def adapt_kernel(which, fresh, turned, *refs):
    teachers = len(turned)
    x_in, refs = refs[0], refs[1:]
    ins, refs = copies_of(refs, 5 * teachers)
    if not fresh:
        refs = refs[4 * teachers :]
    outs, refs = copies_of(refs, 4 * teachers)
    x, refs = refs[0], refs[1:]
    bufs, refs = copies_of(refs, 6 * teachers)
    in_sem, out_sem = refs
    rows = x.shape[0]
    part = 256
    at_out = pl.ds(which * rows, rows)

    first = pltpu.make_async_copy(x_in, x, in_sem.at[5 * teachers])
    first.start()
    loads = []
    for t in range(teachers):
        w1_in, w2o_in, w2s_in, goal_o_in, goal_s_in = ins[5 * t : 5 * t + 5]
        w1, w2, goal = bufs[6 * t : 6 * t + 3]
        if turned[t]:
            width = w2o_in.shape[0]
            w2o, w2s = w2.at[pl.ds(0, width)], w2.at[pl.ds(HALF, width)]
        else:
            width = w2o_in.shape[1]
            w2o, w2s = w2.at[:, pl.ds(0, width)], w2.at[:, pl.ds(HALF, width)]
        pairs = (
            (w1_in, w1),
            (w2o_in, w2o),
            (w2s_in, w2s),
            (goal_o_in.at[at_out], goal.at[:, pl.ds(0, HALF)]),
            (goal_s_in.at[at_out], goal.at[:, pl.ds(HALF, HALF)]),
        )
        group = [
            pltpu.make_async_copy(src, dst, in_sem.at[5 * t + i])
            for i, (src, dst) in enumerate(pairs)
        ]
        for copy in group:
            copy.start()
        loads.append(group)
        if turned[t] and width < HALF:
            zeros = jnp.zeros((HALF - width, w2.shape[1]), bf16)
            w2[width:HALF] = zeros
            w2[HALF + width :] = zeros

    first.wait()
    stores = []

    def send(t, i):
        copy_from = bufs[6 * t + 2 + i]
        target = outs[4 * t + i]
        target = target.at[:, at_out] if i == 3 else target.at[at_out]
        copy = pltpu.make_async_copy(copy_from, target, out_sem.at[4 * t + i])
        copy.start()
        stores.append(copy)

    for t in range(teachers):
        w1, w2, goal, hidden, pred, sums = bufs[6 * t : 6 * t + 6]
        channels = w1.shape[1]
        loads[t][0].wait()
        for m in range(0, rows, part):
            for n in range(0, channels, 512):
                to = min(n + 512, channels)
                hidden[m : m + part, n:to] = gelu(
                    jnp.dot(x[m : m + part], w1[:, n:to], preferred_element_type=f32)
                ).astype(bf16)
        send(t, 1)
        for copy in loads[t][1:]:
            copy.wait()
        send(t, 0)
        for m in range(0, rows, part):
            at = slice(m, m + part)
            p = lax.dot_general(
                hidden[at],
                w2[...],
                (((1,), (1 if turned[t] else 0,)), ((), ())),
                preferred_element_type=f32,
            )
            pred[at] = p
            wide = goal[at].astype(f32)
            pred_sq = jnp.sum(p * p, axis=1, keepdims=True)
            goal_sq = jnp.sum(wide * wide, axis=1, keepdims=True)
            cross = jnp.sum(p * wide, axis=1, keepdims=True)
            lane = lax.broadcasted_iota(jnp.int32, (part, 128), 1)
            cols = jnp.where(lane == 0, pred_sq, jnp.where(lane == 1, goal_sq, cross))
            sums[:, at] = jnp.transpose(cols)[:8]
        send(t, 2)
        send(t, 3)
    for copy in stores:
        copy.wait()


def adapt(x, which, teachers, prior=None):
    rows, width = x.shape
    turned = tuple(w2o.shape[0] != w1.shape[1] for w1, w2o, *_ in teachers)
    outs, scratch = [], [pltpu.VMEM((rows, width), bf16)]
    flops = bytes_ = 0
    for (w1, *_), turn in zip(teachers, turned):
        channels = w1.shape[1]
        wide = 2 * HALF
        outs += [
            jax.ShapeDtypeStruct((2 * rows, wide), bf16),
            jax.ShapeDtypeStruct((2 * rows, channels), bf16),
            jax.ShapeDtypeStruct((2 * rows, wide), f32),
            jax.ShapeDtypeStruct((8, 2 * rows), f32),
        ]
        scratch += [
            pltpu.VMEM(w1.shape, bf16),
            pltpu.VMEM((wide, channels) if turn else (channels, wide), bf16),
            pltpu.VMEM((rows, wide), bf16),
            pltpu.VMEM((rows, channels), bf16),
            pltpu.VMEM((rows, wide), f32),
            pltpu.VMEM((8, rows), f32),
        ]
        flops += 2 * rows * channels * (width + wide)
        bytes_ += 2 * channels * (width + wide + rows)
    n = len(teachers)
    scratch += [pltpu.SemaphoreType.DMA((5 * n + 1,)), pltpu.SemaphoreType.DMA((4 * n,))]
    args = [x] + [a for teacher in teachers for a in teacher]
    aliases = {}
    if prior is not None:
        aliases = {len(args) + i: i for i in range(len(outs))}
        args += list(prior)
    anywhere = pl.BlockSpec(memory_space=pl.ANY)
    return pl.pallas_call(
        functools.partial(adapt_kernel, which, prior is None, turned),
        in_specs=[anywhere] * len(args),
        out_specs=[anywhere] * len(outs),
        out_shape=outs,
        scratch_shapes=scratch,
        input_output_aliases=aliases,
        compiler_params=pltpu.CompilerParams(vmem_limit_bytes=VMEM_LIMIT),
        cost_estimate=pl.CostEstimate(flops=flops, bytes_accessed=bytes_, transcendentals=0),
        name="adapt",
    )(*args)


def shards(
    student,
    dino_feat,
    siglip_feat,
    sam_feat,
    w1_dino,
    w2_dino,
    w1_siglip,
    w2_siglip,
    w1_sam,
    w2_sam,
):
    n_images, row_count, grid, width = student.shape
    n_dp = lax.axis_size("dp")
    g = lax.axis_index("grp")
    total = n_images * n_dp * grid * grid
    own_tokens = n_images * row_count * grid

    own = student.reshape(own_tokens, width)
    theirs = lax.ppermute(own, "grp", CHIP)

    w2s = (w2_dino, jnp.swapaxes(w2_sam, 0, 1), jnp.swapaxes(w2_siglip, 0, 1))
    w2_others = [lax.ppermute(w, "grp", CORE) for w in w2s]

    order = jnp.stack([g ^ 1, g ^ 3, g, g ^ 2]).astype(jnp.int32)
    kept, sent = targets(order, dino_feat, siglip_feat, sam_feat)
    kept = (kept[0], kept[2], kept[1])
    sent = (sent[0], sent[2], sent[1])
    goal_others = [lax.ppermute(s, "grp", CORE) for s in sent]

    teachers = list(zip((w1_dino, w1_sam, w1_siglip), w2s, w2_others, kept, goal_others))
    firsts = adapt(own, 0, teachers)
    states = adapt(theirs, 1, teachers, prior=firsts)
    states = [states[4 * i : 4 * i + 4] for i in range(3)]
    others = [lax.ppermute(s[3], "grp", CHIP) for s in states]

    locals_ = []
    after = None
    for (goal, hidden, pred, part), other in zip(states, others):
        channels = hidden.shape[1]
        scale = channels / math.sqrt(total)
        both = part + jnp.roll(other, own_tokens, axis=1)
        pred_norm = jnp.sqrt(both[0] + epsilon)
        goal_norm = jnp.sqrt(both[1] + epsilon)
        product = pred_norm * goal_norm
        on_goal = -scale / product
        on_pred = scale * both[2] / (product * pred_norm * pred_norm)
        if after is not None:
            on_goal, on_pred, after = lax.optimization_barrier((on_goal, on_pred, after))
        error = (on_goal[:, None] * goal.astype(f32) + on_pred[:, None] * pred).astype(bf16)
        grad = jnp.einsum("tk,tc->kc", hidden, error, preferred_element_type=f32)
        after = grad
        sent_grad = lax.ppermute(grad[:, HALF:].astype(bf16), "grp", CORE)
        grad = grad[:, :HALF] + sent_grad.astype(f32)
        locals_.append(grad.astype(bf16).reshape(n_dp, channels // n_dp, HALF))

    def over_images(parts):
        split = lax.all_to_all(parts, "dp", 0, 0, tiled=True)
        return jnp.sum(split.astype(f32), axis=0)

    dino = over_images(locals_[0])
    rest = over_images(jnp.concatenate(locals_[1:], axis=1))
    sam_rows = locals_[1].shape[1]
    return (
        dino[:, : w2_dino.shape[1]],
        rest[sam_rows:, : w2_siglip.shape[1]],
        rest[:sam_rows, : w2_sam.shape[1]],
    )


def solution(mesh):
    in_specs = (
        P("dp", "grp", None, None),
        P("dp", None, None, "grp"),
        P("dp", None, None, "grp"),
        P("dp", None, None, "grp"),
        P(),
        P(None, "grp"),
        P(),
        P(None, "grp"),
        P(),
        P(None, "grp"),
    )
    out_specs = (P("dp", "grp"), P("dp", "grp"), P("dp", "grp"))
    return jax.shard_map(shards, mesh=mesh, in_specs=in_specs, out_specs=out_specs, check_vma=False)
```

```python
import functools
import math

import jax
import jax.numpy as jnp
from jax import lax
from jax.experimental import pallas as pl
from jax.experimental.pallas import tpu as pltpu
from jax.sharding import PartitionSpec as P

epsilon = 1e-06

f32 = jnp.float32
bf16 = jnp.bfloat16

CORE = [(g, g ^ 1) for g in range(4)]
CHIP = [(g, g ^ 2) for g in range(4)]

HALF = 384
VMEM_LIMIT = 48 * 1024 * 1024


def pad_lanes(x):
    rows, width = x.shape
    if width == HALF:
        return x
    return jnp.concatenate([x, jnp.zeros((rows, HALF - width), x.dtype)], axis=1)


def resample_into(out_ref, at, feat_ref):
    _, in_rows, in_cols, width = feat_ref.shape
    out_rows = in_rows * 8 // 9
    slot = lax.broadcasted_iota(jnp.int32, (8, 1), 0).astype(f32)
    right = 0.125 * slot + 0.0625
    for r in range(out_rows):
        weight = 0.125 * (r % 8) + 0.0625
        first = r // 8 * 9 + r % 8
        row = (1.0 - weight) * feat_ref[0, first].astype(f32) + weight * feat_ref[
            0, first + 1
        ].astype(f32)
        blocks = []
        for b in range(in_cols // 9):
            blocks.append(
                (1.0 - right) * row[9 * b : 9 * b + 8] + right * row[9 * b + 1 : 9 * b + 9]
            )
        done = pad_lanes(jnp.concatenate(blocks, axis=0)).astype(bf16)
        count = done.shape[0]
        out_ref[0, 0, r * count : (r + 1) * count, at * HALF : (at + 1) * HALF] = done


def targets_kernel(order_ref, dino, siglip, sam, kept, sent):
    def fill(out):
        resample_into(out, 0, dino)
        resample_into(out, 2, siglip)
        _, rows, cols, width = sam.shape
        out[0, 0, :, HALF : 2 * HALF] = pad_lanes(sam[0].reshape(rows * cols, width))

    slot = pl.program_id(0)

    @pl.when(slot < 2)
    def _():
        fill(sent)

    @pl.when(slot >= 2)
    def _():
        fill(kept)


def targets(order, dino, siglip, sam):
    n = sam.shape[0]
    run = sam.shape[1] // 4 * sam.shape[2]

    def block_of(feat):
        rows = feat.shape[1] // 4
        return pl.BlockSpec(
            (1, rows) + feat.shape[2:], lambda s, i, order: (i, order[s], 0, 0)
        )

    sent = pl.BlockSpec(
        (1, 1, run, 3 * HALF),
        lambda s, i, order: (jnp.minimum(s, 1), jnp.where(s < 2, i, n - 1), 0, 0),
    )
    kept = pl.BlockSpec(
        (1, 1, run, 3 * HALF),
        lambda s, i, order: (jnp.maximum(s, 2) - 2, jnp.where(s < 2, 0, i), 0, 0),
    )
    outs = pl.pallas_call(
        targets_kernel,
        grid_spec=pltpu.PrefetchScalarGridSpec(
            num_scalar_prefetch=1,
            grid=(4, n),
            in_specs=[block_of(dino), block_of(siglip), block_of(sam)],
            out_specs=[kept, sent],
        ),
        out_shape=[jax.ShapeDtypeStruct((2, n, run, 3 * HALF), bf16)] * 2,
        compiler_params=pltpu.CompilerParams(vmem_limit_bytes=VMEM_LIMIT),
        cost_estimate=pl.CostEstimate(flops=1000, bytes_accessed=1000, transcendentals=0),
        name="targets",
    )(order, dino, siglip, sam)
    return [o.reshape(2 * n * run, 3 * HALF) for o in outs]


def gelu(x):
    inner = x * (0.7978845608028654 + (0.7978845608028654 * 0.044715) * (x * x))
    half = 0.5 * x
    return half + half * jnp.tanh(inner)


def copies_of(refs, n):
    return refs[:n], refs[n:]


def adapt_kernel(which, fresh, turned, pieces, *refs):
    teachers = len(turned)
    x_in, refs = copies_of(refs, pieces)
    (goal_o_in, goal_s_in), refs = copies_of(refs, 2)
    ins, refs = copies_of(refs, 3 * teachers)
    if not fresh:
        refs = refs[3 * teachers + 1 :]
    outs, refs = copies_of(refs, 3 * teachers + 1)
    x, refs = refs[0], refs[1:]
    bufs, refs = copies_of(refs, 5 * teachers)
    sums, in_sem, out_sem = refs
    rows = x.shape[0]
    part = 256
    at_out = pl.ds(which * rows, rows)

    tokens = []
    for i, piece in enumerate(x_in):
        at = sum(p.shape[0] for p in x_in[:i])
        copy = pltpu.make_async_copy(
            piece, x.at[pl.ds(at, piece.shape[0])], in_sem.at[5 * teachers + i]
        )
        copy.start()
        tokens.append(copy)
    loads = []
    for t in range(teachers):
        w1_in, w2o_in, w2s_in = ins[3 * t : 3 * t + 3]
        lanes = pl.ds(t * HALF, HALF)
        w1, w2, goal = bufs[5 * t : 5 * t + 3]
        if turned[t]:
            width = w2o_in.shape[0]
            w2o, w2s = w2.at[pl.ds(0, width)], w2.at[pl.ds(HALF, width)]
        else:
            width = w2o_in.shape[1]
            w2o, w2s = w2.at[:, pl.ds(0, width)], w2.at[:, pl.ds(HALF, width)]
        pairs = (
            (w1_in, w1),
            (w2o_in, w2o),
            (w2s_in, w2s),
            (goal_o_in.at[at_out, lanes], goal.at[:, pl.ds(0, HALF)]),
            (goal_s_in.at[at_out, lanes], goal.at[:, pl.ds(HALF, HALF)]),
        )
        group = [
            pltpu.make_async_copy(src, dst, in_sem.at[5 * t + i])
            for i, (src, dst) in enumerate(pairs)
        ]
        for copy in group:
            copy.start()
        loads.append(group)
        if turned[t] and width < HALF:
            zeros = jnp.zeros((HALF - width, w2.shape[1]), bf16)
            w2[width:HALF] = zeros
            w2[HALF + width :] = zeros

    for copy in tokens:
        copy.wait()
    stores = []

    def send(t, i):
        copy_from = bufs[5 * t + 2 + i]
        target = outs[3 * t + i]
        target = target.at[at_out]
        copy = pltpu.make_async_copy(copy_from, target, out_sem.at[3 * t + i])
        copy.start()
        stores.append(copy)

    for t in range(teachers):
        w1, w2, goal, hidden, pred = bufs[5 * t : 5 * t + 5]
        channels = w1.shape[1]
        loads[t][0].wait()
        for m in range(0, rows, part):
            for n in range(0, channels, 512):
                to = min(n + 512, channels)
                hidden[m : m + part, n:to] = gelu(
                    jnp.dot(x[m : m + part], w1[:, n:to], preferred_element_type=f32)
                ).astype(bf16)
        send(t, 1)
        for copy in loads[t][1:]:
            copy.wait()
        send(t, 0)
        for m in range(0, rows, part):
            at = slice(m, m + part)
            p = lax.dot_general(
                hidden[at],
                w2[...],
                (((1,), (1 if turned[t] else 0,)), ((), ())),
                preferred_element_type=f32,
            )
            pred[at] = p
            wide = goal[at].astype(f32)
            pred_sq = jnp.sum(p * p, axis=1, keepdims=True)
            goal_sq = jnp.sum(wide * wide, axis=1, keepdims=True)
            cross = jnp.sum(p * wide, axis=1, keepdims=True)
            lane = lax.broadcasted_iota(jnp.int32, (part, 128), 1)
            cols = jnp.where(lane == 0, pred_sq, jnp.where(lane == 1, goal_sq, cross))
            sums[8 * t : 8 * t + 8, at] = jnp.transpose(cols)[:8]
        send(t, 2)
    last = pltpu.make_async_copy(sums, outs[3 * teachers].at[:, at_out], out_sem.at[3 * teachers])
    last.start()
    stores.append(last)
    for copy in stores:
        copy.wait()


def adapt(pieces, which, goals, teachers, prior=None):
    rows, width = sum(p.shape[0] for p in pieces), pieces[0].shape[1]
    turned = tuple(w2o.shape[0] != w1.shape[1] for w1, w2o, *_ in teachers)
    outs, scratch = [], [pltpu.VMEM((rows, width), bf16)]
    for (w1, *_), turn in zip(teachers, turned):
        channels = w1.shape[1]
        wide = 2 * HALF
        outs += [
            jax.ShapeDtypeStruct((2 * rows, wide), bf16),
            jax.ShapeDtypeStruct((2 * rows, channels), bf16),
            jax.ShapeDtypeStruct((2 * rows, wide), f32),
        ]
        scratch += [
            pltpu.VMEM(w1.shape, bf16),
            pltpu.VMEM((wide, channels) if turn else (channels, wide), bf16),
            pltpu.VMEM((rows, wide), bf16),
            pltpu.VMEM((rows, channels), bf16),
            pltpu.VMEM((rows, wide), f32),
        ]
    n = len(teachers)
    outs.append(jax.ShapeDtypeStruct((8 * n, 2 * rows), f32))
    scratch += [
        pltpu.VMEM((8 * n, rows), f32),
        pltpu.SemaphoreType.DMA((5 * n + len(pieces),)),
        pltpu.SemaphoreType.DMA((3 * n + 1,)),
    ]
    args = [*pieces, *goals] + [a for teacher in teachers for a in teacher]
    aliases = {}
    if prior is not None:
        aliases = {len(args) + i: i for i in range(len(outs))}
        args += list(prior)
    anywhere = pl.BlockSpec(memory_space=pl.ANY)
    return pl.pallas_call(
        functools.partial(adapt_kernel, which, prior is None, turned, len(pieces)),
        in_specs=[anywhere] * len(args),
        out_specs=[anywhere] * len(outs),
        out_shape=outs,
        scratch_shapes=scratch,
        input_output_aliases=aliases,
        compiler_params=pltpu.CompilerParams(vmem_limit_bytes=VMEM_LIMIT),
        cost_estimate=pl.CostEstimate(flops=1000, bytes_accessed=1000, transcendentals=0),
        name="adapt",
    )(*args)


class Place:
    def __init__(self, index):
        self.at = (index // 8, index // 4 % 2, index % 4)


def swap(value, axis, mask):
    flip = mask * (8, 4, 1)[axis]
    return lax.ppermute(value, "dp", [(d, d ^ flip) for d in range(32)])


def take(value, axis, index):
    return lax.dynamic_index_in_dim(value, index, axis, keepdims=False)


def halved(value, axis, place, dim, masks):
    c = place.at[axis]
    first, second = masks
    out = jnp.stack([take(value, dim, c ^ first), take(value, dim, c ^ first ^ second)])
    got = swap(out.astype(bf16), axis, first).astype(f32)
    mine = take(value, dim, c).astype(f32) + got[0]
    pass_on = take(value, dim, c ^ second).astype(f32) + got[1]
    return mine + swap(pass_on.astype(bf16), axis, second).astype(f32)


def over_images(value, place, axis):
    later = 2 - axis
    parts = []
    for p, masks in enumerate(((1, 3), (3, 1))):
        parts.append(halved(value[:, p], axis, place, 0 if axis == 0 else 1, masks))
    both = jnp.stack(parts)
    c = place.at[later]
    total = take(both, 1, c)
    for mask in (1, 2, 3):
        total = total + swap(take(both, 1, c ^ mask).astype(bf16), later, mask).astype(f32)
    y = place.at[1]
    return take(total, 0, y) + swap(take(total, 0, 1 - y).astype(bf16), 1, 1).astype(f32)


def shards(
    student,
    dino_feat,
    siglip_feat,
    sam_feat,
    w1_dino,
    w2_dino,
    w1_siglip,
    w2_siglip,
    w1_sam,
    w2_sam,
):
    n_images, row_count, grid, width = student.shape
    n_dp = lax.axis_size("dp")
    g = lax.axis_index("grp")
    total = n_images * n_dp * grid * grid
    own_tokens = n_images * row_count * grid

    own = student.reshape(own_tokens, width)
    cut = own_tokens * 3 // 8
    theirs = [lax.ppermute(piece, "grp", CHIP) for piece in (own[:cut], own[cut:])]

    w2s = (w2_dino, jnp.swapaxes(w2_sam, 0, 1), jnp.swapaxes(w2_siglip, 0, 1))
    w2_others = [lax.ppermute(w, "grp", CORE) for w in w2s]

    order = jnp.stack([g ^ 1, g ^ 3, g, g ^ 2]).astype(jnp.int32)
    kept, sent = targets(order, dino_feat, siglip_feat, sam_feat)
    sent, theirs[0] = lax.optimization_barrier((sent, theirs[0]))
    goals = (kept, lax.ppermute(sent, "grp", CORE))

    teachers = list(zip((w1_dino, w1_sam, w1_siglip), w2s, w2_others))
    firsts = adapt([own], 0, goals, teachers)
    states = adapt(theirs, 1, goals, teachers, prior=firsts)
    part = states[9]
    both = part + jnp.roll(lax.ppermute(part, "grp", CHIP), own_tokens, axis=1)

    place = Place(lax.axis_index("dp"))
    locals_ = []
    after = None
    for i in range(3):
        goal, hidden, pred = states[3 * i : 3 * i + 3]
        channels = hidden.shape[1]
        scale = channels / math.sqrt(total)
        pred_norm = jnp.sqrt(both[8 * i] + epsilon)
        goal_norm = jnp.sqrt(both[8 * i + 1] + epsilon)
        product = pred_norm * goal_norm
        on_goal = -scale / product
        on_pred = scale * both[8 * i + 2] / (product * pred_norm * pred_norm)
        if after is not None:
            on_goal, on_pred, after = lax.optimization_barrier((on_goal, on_pred, after))
        error = (on_goal[:, None] * goal.astype(f32) + on_pred[:, None] * pred).astype(bf16)
        grad = jnp.einsum("tk,tc->kc", hidden, error, preferred_element_type=f32)
        after = grad
        sent_grad = lax.ppermute(grad[:, HALF:].astype(bf16), "grp", CORE)
        grad = grad[:, :HALF] + sent_grad.astype(f32)
        locals_.append(grad.astype(bf16).reshape(4, 2, 4, channels // n_dp, HALF))

    dino = over_images(locals_[0], place, 0)
    rest = over_images(jnp.concatenate(locals_[1:], axis=3), place, 2)
    sam_rows = locals_[1].shape[3]
    return (
        dino[:, : w2_dino.shape[1]],
        rest[sam_rows:, : w2_siglip.shape[1]],
        rest[:sam_rows, : w2_sam.shape[1]],
    )


def solution(mesh):
    in_specs = (
        P("dp", "grp", None, None),
        P("dp", None, None, "grp"),
        P("dp", None, None, "grp"),
        P("dp", None, None, "grp"),
        P(),
        P(None, "grp"),
        P(),
        P(None, "grp"),
        P(),
        P(None, "grp"),
    )
    out_specs = (P("dp", "grp"), P("dp", "grp"), P("dp", "grp"))
    return jax.shard_map(shards, mesh=mesh, in_specs=in_specs, out_specs=out_specs, check_vma=False)
```

```python
import functools
import math

import jax
import jax.numpy as jnp
from jax import lax
from jax.experimental import pallas as pl
from jax.experimental.pallas import tpu as pltpu
from jax.sharding import PartitionSpec as P

epsilon = 1e-06

f32 = jnp.float32
bf16 = jnp.bfloat16

CORE = [(g, g ^ 1) for g in range(4)]
CHIP = [(g, g ^ 2) for g in range(4)]

HALF = 384
MIB = 1024 * 1024


def pad_lanes(x):
    rows, width = x.shape
    if width == HALF:
        return x
    return jnp.concatenate([x, jnp.zeros((rows, HALF - width), x.dtype)], axis=1)


def resample_into(out_ref, at, feat_ref):
    _, in_rows, in_cols, width = feat_ref.shape
    out_rows = in_rows * 8 // 9
    slot = lax.broadcasted_iota(jnp.int32, (8, 1), 0).astype(f32)
    right = 0.125 * slot + 0.0625
    for r in range(out_rows):
        weight = 0.125 * (r % 8) + 0.0625
        first = r // 8 * 9 + r % 8
        row = (1.0 - weight) * feat_ref[0, first].astype(f32) + weight * feat_ref[
            0, first + 1
        ].astype(f32)
        blocks = []
        for b in range(in_cols // 9):
            blocks.append(
                (1.0 - right) * row[9 * b : 9 * b + 8] + right * row[9 * b + 1 : 9 * b + 9]
            )
        done = pad_lanes(jnp.concatenate(blocks, axis=0)).astype(bf16)
        count = done.shape[0]
        out_ref[0, 0, r * count : (r + 1) * count, at * HALF : (at + 1) * HALF] = done


def targets_kernel(order_ref, dino, siglip, sam, kept, sent):
    def fill(out):
        resample_into(out, 0, dino)
        resample_into(out, 2, siglip)
        _, rows, cols, width = sam.shape
        out[0, 0, :, HALF : 2 * HALF] = pad_lanes(sam[0].reshape(rows * cols, width))

    slot = pl.program_id(0)

    @pl.when(slot < 2)
    def _():
        fill(sent)

    @pl.when(slot >= 2)
    def _():
        fill(kept)


def targets(order, dino, siglip, sam):
    n = sam.shape[0]
    run = sam.shape[1] // 4 * sam.shape[2]

    def block_of(feat):
        rows = feat.shape[1] // 4
        return pl.BlockSpec(
            (1, rows) + feat.shape[2:], lambda s, i, order: (i, order[s], 0, 0)
        )

    sent = pl.BlockSpec(
        (1, 1, run, 3 * HALF),
        lambda s, i, order: (jnp.minimum(s, 1), jnp.where(s < 2, i, n - 1), 0, 0),
    )
    kept = pl.BlockSpec(
        (1, 1, run, 3 * HALF),
        lambda s, i, order: (jnp.maximum(s, 2) - 2, jnp.where(s < 2, 0, i), 0, 0),
    )
    outs = pl.pallas_call(
        targets_kernel,
        grid_spec=pltpu.PrefetchScalarGridSpec(
            num_scalar_prefetch=1,
            grid=(4, n),
            in_specs=[block_of(dino), block_of(siglip), block_of(sam)],
            out_specs=[kept, sent],
        ),
        out_shape=[jax.ShapeDtypeStruct((2, n, run, 3 * HALF), bf16)] * 2,
        compiler_params=pltpu.CompilerParams(vmem_limit_bytes=12 * MIB),
        cost_estimate=pl.CostEstimate(flops=1000, bytes_accessed=1000, transcendentals=0),
        name="targets",
    )(order, dino, siglip, sam)
    return [o.reshape(2 * n * run, 3 * HALF) for o in outs]


def gelu(x):
    inner = x * (0.7978845608028654 + (0.7978845608028654 * 0.044715) * (x * x))
    half = 0.5 * x
    return half + half * jnp.tanh(inner)


def copies_of(refs, n):
    return refs[:n], refs[n:]


def adapt_kernel(which, fresh, turned, slots, pieces, *refs):
    teachers = len(turned)
    x_in, refs = copies_of(refs, pieces)
    (goal_o_in, goal_s_in), refs = copies_of(refs, 2)
    ins, refs = copies_of(refs, 3 * teachers)
    if not fresh:
        refs = refs[4 * teachers :]
    outs, refs = copies_of(refs, 4 * teachers)
    x, refs = refs[0], refs[1:]
    bufs, refs = copies_of(refs, 6 * teachers)
    in_sem, out_sem = refs
    rows = x.shape[0]
    part = 256
    at_out = pl.ds(which * rows, rows)

    tokens = []
    for i, piece in enumerate(x_in):
        at = sum(p.shape[0] for p in x_in[:i])
        copy = pltpu.make_async_copy(
            piece, x.at[pl.ds(at, piece.shape[0])], in_sem.at[5 * teachers + i]
        )
        copy.start()
        tokens.append(copy)
    loads = []
    for t in range(teachers):
        w1_in, w2o_in, w2s_in = ins[3 * t : 3 * t + 3]
        lanes = pl.ds(slots[t] * HALF, HALF)
        w1, w2, goal = bufs[6 * t : 6 * t + 3]
        if turned[t]:
            width = w2o_in.shape[0]
            w2o, w2s = w2.at[pl.ds(0, width)], w2.at[pl.ds(HALF, width)]
        else:
            width = w2o_in.shape[1]
            w2o, w2s = w2.at[:, pl.ds(0, width)], w2.at[:, pl.ds(HALF, width)]
        pairs = (
            (w1_in, w1),
            (w2o_in, w2o),
            (w2s_in, w2s),
            (goal_o_in.at[at_out, lanes], goal.at[:, pl.ds(0, HALF)]),
            (goal_s_in.at[at_out, lanes], goal.at[:, pl.ds(HALF, HALF)]),
        )
        group = [
            pltpu.make_async_copy(src, dst, in_sem.at[5 * t + i])
            for i, (src, dst) in enumerate(pairs)
        ]
        for copy in group:
            copy.start()
        loads.append(group)
        if turned[t] and width < HALF:
            zeros = jnp.zeros((HALF - width, w2.shape[1]), bf16)
            w2[width:HALF] = zeros
            w2[HALF + width :] = zeros

    for copy in tokens:
        copy.wait()
    stores = []

    def send(t, i):
        copy_from = bufs[6 * t + 2 + i]
        target = outs[4 * t + i]
        target = target.at[:, at_out] if i == 3 else target.at[at_out]
        copy = pltpu.make_async_copy(copy_from, target, out_sem.at[4 * t + i])
        copy.start()
        stores.append(copy)

    for t in range(teachers):
        w1, w2, goal, hidden, pred, sums = bufs[6 * t : 6 * t + 6]
        channels = w1.shape[1]
        loads[t][0].wait()
        for m in range(0, rows, part):
            for n in range(0, channels, 512):
                to = min(n + 512, channels)
                hidden[m : m + part, n:to] = gelu(
                    jnp.dot(x[m : m + part], w1[:, n:to], preferred_element_type=f32)
                ).astype(bf16)
        send(t, 1)
        for copy in loads[t][1:]:
            copy.wait()
        send(t, 0)
        for m in range(0, rows, part):
            at = slice(m, m + part)
            p = lax.dot_general(
                hidden[at],
                w2[...],
                (((1,), (1 if turned[t] else 0,)), ((), ())),
                preferred_element_type=f32,
            )
            pred[at] = p
            wide = goal[at].astype(f32)
            pred_sq = jnp.sum(p * p, axis=1, keepdims=True)
            goal_sq = jnp.sum(wide * wide, axis=1, keepdims=True)
            cross = jnp.sum(p * wide, axis=1, keepdims=True)
            lane = lax.broadcasted_iota(jnp.int32, (part, 128), 1)
            cols = jnp.where(lane == 0, pred_sq, jnp.where(lane == 1, goal_sq, cross))
            sums[:, at] = jnp.transpose(cols)[:8]
        send(t, 2)
        send(t, 3)
    for copy in stores:
        copy.wait()


def adapt(pieces, which, goals, teachers, slots, prior=None):
    rows, width = sum(p.shape[0] for p in pieces), pieces[0].shape[1]
    turned = tuple(w2o.shape[0] != w1.shape[1] for w1, w2o, *_ in teachers)
    outs, scratch = [], [pltpu.VMEM((rows, width), bf16)]
    for (w1, *_), turn in zip(teachers, turned):
        channels = w1.shape[1]
        wide = 2 * HALF
        outs += [
            jax.ShapeDtypeStruct((2 * rows, wide), bf16),
            jax.ShapeDtypeStruct((2 * rows, channels), bf16),
            jax.ShapeDtypeStruct((2 * rows, wide), f32),
            jax.ShapeDtypeStruct((8, 2 * rows), f32),
        ]
        scratch += [
            pltpu.VMEM(w1.shape, bf16),
            pltpu.VMEM((wide, channels) if turn else (channels, wide), bf16),
            pltpu.VMEM((rows, wide), bf16),
            pltpu.VMEM((rows, channels), bf16),
            pltpu.VMEM((rows, wide), f32),
            pltpu.VMEM((8, rows), f32),
        ]
    n = len(teachers)
    held = sum(math.prod(b.shape) * jnp.dtype(b.dtype).itemsize for b in scratch)
    scratch += [
        pltpu.SemaphoreType.DMA((5 * n + len(pieces),)),
        pltpu.SemaphoreType.DMA((4 * n,)),
    ]
    args = [*pieces, *goals] + [a for teacher in teachers for a in teacher]
    aliases = {}
    if prior is not None:
        aliases = {len(args) + i: i for i in range(len(outs))}
        args += list(prior)
    anywhere = pl.BlockSpec(memory_space=pl.ANY)
    return pl.pallas_call(
        functools.partial(adapt_kernel, which, prior is None, turned, slots, len(pieces)),
        in_specs=[anywhere] * len(args),
        out_specs=[anywhere] * len(outs),
        out_shape=outs,
        scratch_shapes=scratch,
        input_output_aliases=aliases,
        compiler_params=pltpu.CompilerParams(vmem_limit_bytes=held + 3 * MIB),
        cost_estimate=pl.CostEstimate(flops=1000, bytes_accessed=1000, transcendentals=0),
        name="adapt",
    )(*args)


def shards(
    student,
    dino_feat,
    siglip_feat,
    sam_feat,
    w1_dino,
    w2_dino,
    w1_siglip,
    w2_siglip,
    w1_sam,
    w2_sam,
):
    n_images, row_count, grid, width = student.shape
    n_dp = lax.axis_size("dp")
    g = lax.axis_index("grp")
    total = n_images * n_dp * grid * grid
    own_tokens = n_images * row_count * grid

    own = student.reshape(own_tokens, width)
    cut = own_tokens * 3 // 8
    theirs = [lax.ppermute(piece, "grp", CHIP) for piece in (own[:cut], own[cut:])]

    w2s = (w2_dino, jnp.swapaxes(w2_sam, 0, 1), jnp.swapaxes(w2_siglip, 0, 1))
    w2_others = [lax.ppermute(w, "grp", CORE) for w in w2s]

    order = jnp.stack([g ^ 1, g ^ 3, g, g ^ 2]).astype(jnp.int32)
    kept, sent = targets(order, dino_feat, siglip_feat, sam_feat)
    sent, theirs[0], *w2_others = lax.optimization_barrier((sent, theirs[0], *w2_others))
    goals = (kept, lax.ppermute(sent, "grp", CORE))

    teachers = list(zip((w1_dino, w1_sam, w1_siglip), w2s, w2_others))
    firsts = adapt([own], 0, goals, teachers, (0, 1, 2))

    def second(i, after):
        pieces = list(theirs)
        if after is not None:
            *pieces, after = lax.optimization_barrier((*pieces, after))
        return adapt(pieces, 1, goals, teachers[i : i + 1], (i,), firsts[4 * i : 4 * i + 4])

    def gradient(state, after):
        goal, hidden, pred, part = state
        channels = hidden.shape[1]
        scale = channels / math.sqrt(total)
        sums = part + jnp.roll(lax.ppermute(part, "grp", CHIP), own_tokens, axis=1)
        pred_norm = jnp.sqrt(sums[0] + epsilon)
        goal_norm = jnp.sqrt(sums[1] + epsilon)
        product = pred_norm * goal_norm
        on_goal = -scale / product
        on_pred = scale * sums[2] / (product * pred_norm * pred_norm)
        on_goal, on_pred, after = lax.optimization_barrier((on_goal, on_pred, after))
        error = (on_goal[:, None] * goal.astype(f32) + on_pred[:, None] * pred).astype(bf16)
        return jnp.einsum("tk,tc->kc", hidden, error, preferred_element_type=f32)

    def between_cores(grad):
        sent_grad = lax.ppermute(grad[:, HALF:].astype(bf16), "grp", CORE)
        both = (grad[:, :HALF] + sent_grad.astype(f32)).astype(bf16)
        return both.reshape(n_dp, both.shape[0] // n_dp, HALF)

    def over_images(parts):
        split = lax.all_to_all(parts, "dp", 0, 0, tiled=True)
        return jnp.sum(split.astype(f32), axis=0)

    dino_state = second(0, None)
    sam_state = second(1, dino_state[3])
    dino_grad = gradient(dino_state, sam_state[3])
    siglip_state = second(2, dino_grad)
    dino_local = between_cores(dino_grad)
    sam_grad = gradient(sam_state, (dino_local, siglip_state[3]))
    siglip_grad = gradient(siglip_state, sam_grad)
    dino = over_images(dino_local)

    sam_local, siglip_local = between_cores(sam_grad), between_cores(siglip_grad)
    sam_width, siglip_width = w2_sam.shape[1], w2_siglip.shape[1]
    sam_rows, siglip_rows = sam_local.shape[1], siglip_local.shape[1]
    siglip_local = jnp.pad(siglip_local, ((0, 0), (0, sam_rows - siglip_rows), (0, 0)))
    rest = over_images(
        jnp.concatenate(
            [
                sam_local[..., :256],
                siglip_local[..., :256],
                sam_local[..., 256:sam_width],
                siglip_local[..., 256:siglip_width],
            ],
            axis=2,
        )
    )
    sam = jnp.concatenate([rest[:, :256], rest[:, 512 : 256 + sam_width]], axis=1)
    siglip = jnp.concatenate([rest[:, 256:512], rest[:, 256 + sam_width :]], axis=1)
    return dino, siglip[:siglip_rows], sam


def solution(mesh):
    in_specs = (
        P("dp", "grp", None, None),
        P("dp", None, None, "grp"),
        P("dp", None, None, "grp"),
        P("dp", None, None, "grp"),
        P(),
        P(None, "grp"),
        P(),
        P(None, "grp"),
        P(),
        P(None, "grp"),
    )
    out_specs = (P("dp", "grp"), P("dp", "grp"), P("dp", "grp"))
    return jax.shard_map(shards, mesh=mesh, in_specs=in_specs, out_specs=out_specs, check_vma=False)
```

```python
import functools
import math

import jax
import jax.numpy as jnp
from jax import lax
from jax.experimental import pallas as pl
from jax.experimental.pallas import tpu as pltpu
from jax.sharding import PartitionSpec as P

epsilon = 1e-06

f32 = jnp.float32
bf16 = jnp.bfloat16

CORE = [(g, g ^ 1) for g in range(4)]
CHIP = [(g, g ^ 2) for g in range(4)]

HALF = 384
MIB = 1024 * 1024


def pad_lanes(x):
    rows, width = x.shape
    if width == HALF:
        return x
    return jnp.concatenate([x, jnp.zeros((rows, HALF - width), x.dtype)], axis=1)


def resample_into(out_ref, at, feat_ref):
    _, in_rows, in_cols, width = feat_ref.shape
    out_rows = in_rows * 8 // 9
    slot = lax.broadcasted_iota(jnp.int32, (8, 1), 0).astype(f32)
    right = 0.125 * slot + 0.0625
    for r in range(out_rows):
        weight = 0.125 * (r % 8) + 0.0625
        first = r // 8 * 9 + r % 8
        row = (1.0 - weight) * feat_ref[0, first].astype(f32) + weight * feat_ref[
            0, first + 1
        ].astype(f32)
        blocks = []
        for b in range(in_cols // 9):
            blocks.append(
                (1.0 - right) * row[9 * b : 9 * b + 8] + right * row[9 * b + 1 : 9 * b + 9]
            )
        done = pad_lanes(jnp.concatenate(blocks, axis=0)).astype(bf16)
        count = done.shape[0]
        out_ref[0, 0, r * count : (r + 1) * count, at * HALF : (at + 1) * HALF] = done


def targets_kernel(order_ref, dino, siglip, sam, kept, sent):
    def fill(out):
        resample_into(out, 0, dino)
        resample_into(out, 2, siglip)
        _, rows, cols, width = sam.shape
        out[0, 0, :, HALF : 2 * HALF] = pad_lanes(sam[0].reshape(rows * cols, width))

    slot = pl.program_id(0)

    @pl.when(slot < 2)
    def _():
        fill(sent)

    @pl.when(slot >= 2)
    def _():
        fill(kept)


def targets(order, dino, siglip, sam):
    n = sam.shape[0]
    run = sam.shape[1] // 4 * sam.shape[2]

    def block_of(feat):
        rows = feat.shape[1] // 4
        return pl.BlockSpec(
            (1, rows) + feat.shape[2:], lambda s, i, order: (i, order[s], 0, 0)
        )

    sent = pl.BlockSpec(
        (1, 1, run, 3 * HALF),
        lambda s, i, order: (jnp.minimum(s, 1), jnp.where(s < 2, i, n - 1), 0, 0),
    )
    kept = pl.BlockSpec(
        (1, 1, run, 3 * HALF),
        lambda s, i, order: (jnp.maximum(s, 2) - 2, jnp.where(s < 2, 0, i), 0, 0),
    )
    outs = pl.pallas_call(
        targets_kernel,
        grid_spec=pltpu.PrefetchScalarGridSpec(
            num_scalar_prefetch=1,
            grid=(4, n),
            in_specs=[block_of(dino), block_of(siglip), block_of(sam)],
            out_specs=[kept, sent],
        ),
        out_shape=[jax.ShapeDtypeStruct((2, n, run, 3 * HALF), bf16)] * 2,
        compiler_params=pltpu.CompilerParams(vmem_limit_bytes=12 * MIB),
        cost_estimate=pl.CostEstimate(flops=1000, bytes_accessed=1000, transcendentals=0),
        name="targets",
    )(order, dino, siglip, sam)
    return [o.reshape(2 * n * run, 3 * HALF) for o in outs]


def gelu(x):
    inner = x * (0.7978845608028654 + (0.7978845608028654 * 0.044715) * (x * x))
    half = 0.5 * x
    return half + half * jnp.tanh(inner)


def column_runs(channels):
    return [(n, min(n + 512, channels)) for n in range(0, channels, 512)]


def copies_of(refs, n):
    return refs[:n], refs[n:]


def adapt_kernel(which, fresh, turned, slots, pieces, *refs):
    teachers = len(turned)
    x_in, refs = copies_of(refs, pieces)
    (goal_o_in, goal_s_in), refs = copies_of(refs, 2)
    ins, refs = copies_of(refs, 3 * teachers)
    if not fresh:
        refs = refs[4 * teachers :]
    outs, refs = copies_of(refs, 4 * teachers)
    x, refs = refs[0], refs[1:]
    bufs, refs = copies_of(refs, 6 * teachers)
    in_sem, w1_sem, out_sem = refs
    rows = x.shape[0]
    part = 256
    at_out = pl.ds(which * rows, rows)

    tokens = []
    for i, piece in enumerate(x_in):
        at = sum(p.shape[0] for p in x_in[:i])
        copy = pltpu.make_async_copy(
            piece, x.at[pl.ds(at, piece.shape[0])], in_sem.at[5 * teachers + i]
        )
        copy.start()
        tokens.append(copy)
    loads = []
    for t in range(teachers):
        w1_in, w2o_in, w2s_in = ins[3 * t : 3 * t + 3]
        lanes = pl.ds(slots[t] * HALF, HALF)
        w1, w2, goal = bufs[6 * t : 6 * t + 3]
        if turned[t]:
            width = w2o_in.shape[0]
            w2o, w2s = w2.at[pl.ds(0, width)], w2.at[pl.ds(HALF, width)]
        else:
            width = w2o_in.shape[1]
            w2o, w2s = w2.at[:, pl.ds(0, width)], w2.at[:, pl.ds(HALF, width)]
        strips = [
            pltpu.make_async_copy(
                w1_in.at[:, pl.ds(n, to - n)],
                w1.at[:, pl.ds(n, to - n)],
                w1_sem.at[4 * t + i],
            )
            for i, (n, to) in enumerate(column_runs(w1.shape[1]))
        ]
        pairs = (
            (w2o_in, w2o),
            (w2s_in, w2s),
            (goal_o_in.at[at_out, lanes], goal.at[:, pl.ds(0, HALF)]),
            (goal_s_in.at[at_out, lanes], goal.at[:, pl.ds(HALF, HALF)]),
        )
        group = [
            pltpu.make_async_copy(src, dst, in_sem.at[5 * t + i])
            for i, (src, dst) in enumerate(pairs)
        ]
        for copy in strips + group:
            copy.start()
        loads.append((strips, group))
        if turned[t] and width < HALF:
            zeros = jnp.zeros((HALF - width, w2.shape[1]), bf16)
            w2[width:HALF] = zeros
            w2[HALF + width :] = zeros

    for copy in tokens:
        copy.wait()
    stores = []

    def send(t, i):
        copy_from = bufs[6 * t + 2 + i]
        target = outs[4 * t + i]
        target = target.at[:, at_out] if i == 3 else target.at[at_out]
        copy = pltpu.make_async_copy(copy_from, target, out_sem.at[4 * t + i])
        copy.start()
        stores.append(copy)

    for t in range(teachers):
        w1, w2, goal, hidden, pred, sums = bufs[6 * t : 6 * t + 6]
        channels = w1.shape[1]
        strips, group = loads[t]
        for strip, (n, to) in zip(strips, column_runs(channels)):
            strip.wait()
            for m in range(0, rows, part):
                hidden[m : m + part, n:to] = gelu(
                    jnp.dot(x[m : m + part], w1[:, n:to], preferred_element_type=f32)
                ).astype(bf16)
        send(t, 1)
        for copy in group:
            copy.wait()
        send(t, 0)
        for m in range(0, rows, part):
            at = slice(m, m + part)
            p = lax.dot_general(
                hidden[at],
                w2[...],
                (((1,), (1 if turned[t] else 0,)), ((), ())),
                preferred_element_type=f32,
            )
            pred[at] = p
            wide = goal[at].astype(f32)
            pred_sq = jnp.sum(p * p, axis=1, keepdims=True)
            goal_sq = jnp.sum(wide * wide, axis=1, keepdims=True)
            cross = jnp.sum(p * wide, axis=1, keepdims=True)
            lane = lax.broadcasted_iota(jnp.int32, (part, 128), 1)
            cols = jnp.where(lane == 0, pred_sq, jnp.where(lane == 1, goal_sq, cross))
            sums[:, at] = jnp.transpose(cols)[:8]
        send(t, 2)
        send(t, 3)
    for copy in stores:
        copy.wait()


def adapt(pieces, which, goals, teachers, slots, prior=None):
    rows, width = sum(p.shape[0] for p in pieces), pieces[0].shape[1]
    turned = tuple(w2o.shape[0] != w1.shape[1] for w1, w2o, *_ in teachers)
    outs, scratch = [], [pltpu.VMEM((rows, width), bf16)]
    for (w1, *_), turn in zip(teachers, turned):
        channels = w1.shape[1]
        wide = 2 * HALF
        outs += [
            jax.ShapeDtypeStruct((2 * rows, wide), bf16),
            jax.ShapeDtypeStruct((2 * rows, channels), bf16),
            jax.ShapeDtypeStruct((2 * rows, wide), f32),
            jax.ShapeDtypeStruct((8, 2 * rows), f32),
        ]
        scratch += [
            pltpu.VMEM(w1.shape, bf16),
            pltpu.VMEM((wide, channels) if turn else (channels, wide), bf16),
            pltpu.VMEM((rows, wide), bf16),
            pltpu.VMEM((rows, channels), bf16),
            pltpu.VMEM((rows, wide), f32),
            pltpu.VMEM((8, rows), f32),
        ]
    n = len(teachers)
    held = sum(math.prod(b.shape) * jnp.dtype(b.dtype).itemsize for b in scratch)
    scratch += [
        pltpu.SemaphoreType.DMA((5 * n + len(pieces),)),
        pltpu.SemaphoreType.DMA((4 * n,)),
        pltpu.SemaphoreType.DMA((4 * n,)),
    ]
    args = [*pieces, *goals] + [a for teacher in teachers for a in teacher]
    aliases = {}
    if prior is not None:
        aliases = {len(args) + i: i for i in range(len(outs))}
        args += list(prior)
    anywhere = pl.BlockSpec(memory_space=pl.ANY)
    return pl.pallas_call(
        functools.partial(adapt_kernel, which, prior is None, turned, slots, len(pieces)),
        in_specs=[anywhere] * len(args),
        out_specs=[anywhere] * len(outs),
        out_shape=outs,
        scratch_shapes=scratch,
        input_output_aliases=aliases,
        compiler_params=pltpu.CompilerParams(vmem_limit_bytes=max(held + 3 * MIB, 44 * MIB)),
        cost_estimate=pl.CostEstimate(flops=1000, bytes_accessed=1000, transcendentals=0),
        name="adapt",
    )(*args)


def pack_kernel(blocks, dino, dino_other, sam, sam_other, siglip, siglip_other, out):
    sums = [
        a[...].astype(f32) + b[...].astype(f32)
        for a, b in ((dino, dino_other), (sam, sam_other), (siglip, siglip_other))
    ]
    rows = [total.shape[0] // blocks for total in sums]
    tall = rows[1]
    for j in range(blocks):
        d, m, s = [total[j * r : (j + 1) * r] for total, r in zip(sums, rows)]
        s = jnp.concatenate([s, jnp.zeros((tall - rows[2], HALF), f32)], axis=0)
        mixed = m[:, 256:] + pltpu.roll(s[:, 256:], 64, 1)
        strips = [d[:, :128], d[:, 128:256], d[:, 256:], m[:, :128], m[:, 128:256], mixed]
        strips += [s[:, :128], s[:, 128:256]]
        count = sum(strip.shape[0] for strip in strips)
        strips.append(jnp.zeros((out.shape[1] - count, 128), f32))
        out[j] = jnp.concatenate(strips, axis=0).astype(bf16)


def pack(grads, received, n_dp):
    blocks = 4
    steps = n_dp // blocks
    rows = [g.shape[0] // n_dp for g in grads]
    height = -(-(3 * rows[0] + 5 * rows[1]) // 16) * 16
    args, specs = [], []
    for grad, other, r in zip(grads, received, rows):
        args += [grad, other]
        specs += [pl.BlockSpec((r * blocks, HALF), lambda i: (i, 0))] * 2
    return pl.pallas_call(
        functools.partial(pack_kernel, blocks),
        grid=(steps,),
        in_specs=specs,
        out_specs=pl.BlockSpec((blocks, height, 128), lambda i: (i, 0, 0)),
        out_shape=jax.ShapeDtypeStruct((n_dp, height, 128), bf16),
        compiler_params=pltpu.CompilerParams(vmem_limit_bytes=16 * MIB),
        name="pack",
    )(*args)


def unpack(total, rows):
    dino, sam, siglip = rows
    at = 3 * dino
    mixed = total[at + 2 * sam : at + 3 * sam]
    low = at + 3 * sam
    return (
        jnp.concatenate([total[i * dino : (i + 1) * dino] for i in range(3)], axis=1),
        jnp.concatenate([total[low : low + siglip], total[low + sam : low + sam + siglip], mixed[:siglip, 64:96]], axis=1),
        jnp.concatenate([total[at : at + sam], total[at + sam : at + 2 * sam], mixed[:, :64]], axis=1),
    )


def shards(
    student,
    dino_feat,
    siglip_feat,
    sam_feat,
    w1_dino,
    w2_dino,
    w1_siglip,
    w2_siglip,
    w1_sam,
    w2_sam,
):
    n_images, row_count, grid, width = student.shape
    n_dp = lax.axis_size("dp")
    g = lax.axis_index("grp")
    total = n_images * n_dp * grid * grid
    own_tokens = n_images * row_count * grid

    own = student.reshape(own_tokens, width)
    cut = own_tokens // 4
    theirs = [lax.ppermute(piece, "grp", CHIP) for piece in (own[:cut], own[cut:])]

    w2s = (w2_dino, jnp.swapaxes(w2_sam, 0, 1), jnp.swapaxes(w2_siglip, 0, 1))
    w2_others = [lax.ppermute(w, "grp", CORE) for w in w2s]

    order = jnp.stack([g ^ 1, g ^ 3, g, g ^ 2]).astype(jnp.int32)
    kept, sent = targets(order, dino_feat, siglip_feat, sam_feat)
    sent, theirs[0], *w2_others = lax.optimization_barrier((sent, theirs[0], *w2_others))
    goals = (kept, lax.ppermute(sent, "grp", CORE))

    teachers = list(zip((w1_dino, w1_sam, w1_siglip), w2s, w2_others))
    firsts = adapt([own], 0, goals, teachers, (0, 1, 2))

    def second(i, to, after=None):
        pieces = list(theirs)
        if after is not None:
            *pieces, after = lax.optimization_barrier((*pieces, after))
        slots = tuple(range(i, to))
        return adapt(pieces, 1, goals, teachers[i:to], slots, firsts[4 * i : 4 * to])

    def gradient(state, after):
        goal, hidden, pred, part = state
        channels = hidden.shape[1]
        scale = channels / math.sqrt(total)
        sums = part + jnp.roll(lax.ppermute(part, "grp", CHIP), own_tokens, axis=1)
        pred_norm = jnp.sqrt(sums[0] + epsilon)
        goal_norm = jnp.sqrt(sums[1] + epsilon)
        product = pred_norm * goal_norm
        on_goal = -scale / product
        on_pred = scale * sums[2] / (product * pred_norm * pred_norm)
        on_goal, on_pred, after = lax.optimization_barrier((on_goal, on_pred, after))
        error = (on_goal[:, None] * goal.astype(f32) + on_pred[:, None] * pred).astype(bf16)
        grad = jnp.einsum("tk,tc->kc", hidden, error, preferred_element_type=f32)
        return grad.astype(bf16)

    dino_state = second(0, 1)
    others = second(1, 3, dino_state[3])
    sam_state, siglip_state = others[:4], others[4:]
    grads = [gradient(dino_state, sam_state[3])]
    grads.append(gradient(sam_state, grads[0]))
    grads.append(gradient(siglip_state, grads[1]))
    received = [lax.ppermute(grad[:, HALF:], "grp", CORE) for grad in grads]
    split = lax.all_to_all(pack(grads, received, n_dp), "dp", 0, 0, tiled=True)
    return unpack(
        jnp.sum(split.astype(f32), axis=0), [w.shape[0] // n_dp for w in (w2_dino, w2_sam, w2_siglip)]
    )


def solution(mesh):
    in_specs = (
        P("dp", "grp", None, None),
        P("dp", None, None, "grp"),
        P("dp", None, None, "grp"),
        P("dp", None, None, "grp"),
        P(),
        P(None, "grp"),
        P(),
        P(None, "grp"),
        P(),
        P(None, "grp"),
    )
    out_specs = (P("dp", "grp"), P("dp", "grp"), P("dp", "grp"))
    return jax.shard_map(shards, mesh=mesh, in_specs=in_specs, out_specs=out_specs, check_vma=False)
```

```python
import functools
import math

import jax
import jax.numpy as jnp
from jax import lax
from jax.experimental import pallas as pl
from jax.experimental.pallas import tpu as pltpu
from jax.sharding import PartitionSpec as P

epsilon = 1e-06

f32 = jnp.float32
bf16 = jnp.bfloat16

CORE = [(g, g ^ 1) for g in range(4)]
CHIP = [(g, g ^ 2) for g in range(4)]

HALF = 384
MIB = 1024 * 1024

AHEAD = 4


def pad_lanes(x):
    rows, width = x.shape
    if width == HALF:
        return x
    return jnp.concatenate([x, jnp.zeros((rows, HALF - width), x.dtype)], axis=1)


def resample_into(out_ref, at, feat_ref):
    _, in_rows, in_cols, width = feat_ref.shape
    out_rows = in_rows * 8 // 9
    slot = lax.broadcasted_iota(jnp.int32, (8, 1), 0).astype(f32)
    right = 0.125 * slot + 0.0625
    for r in range(out_rows):
        weight = 0.125 * (r % 8) + 0.0625
        first = r // 8 * 9 + r % 8
        row = (1.0 - weight) * feat_ref[0, first].astype(f32) + weight * feat_ref[
            0, first + 1
        ].astype(f32)
        blocks = []
        for b in range(in_cols // 9):
            blocks.append(
                (1.0 - right) * row[9 * b : 9 * b + 8] + right * row[9 * b + 1 : 9 * b + 9]
            )
        done = pad_lanes(jnp.concatenate(blocks, axis=0)).astype(bf16)
        count = done.shape[0]
        out_ref[0, 0, r * count : (r + 1) * count, at * HALF : (at + 1) * HALF] = done


def targets_kernel(order_ref, dino, siglip, sam, kept, sent):
    def fill(out):
        resample_into(out, 0, dino)
        resample_into(out, 2, siglip)
        _, rows, cols, width = sam.shape
        out[0, 0, :, HALF : 2 * HALF] = pad_lanes(sam[0].reshape(rows * cols, width))

    slot = pl.program_id(0)

    @pl.when(slot < 2)
    def _():
        fill(sent)

    @pl.when(slot >= 2)
    def _():
        fill(kept)


def targets(order, dino, siglip, sam):
    n = sam.shape[0]
    run = sam.shape[1] // 4 * sam.shape[2]

    def block_of(feat):
        rows = feat.shape[1] // 4
        return pl.BlockSpec(
            (1, rows) + feat.shape[2:], lambda s, i, order: (i, order[s], 0, 0)
        )

    sent = pl.BlockSpec(
        (1, 1, run, 3 * HALF),
        lambda s, i, order: (jnp.minimum(s, 1), jnp.where(s < 2, i, n - 1), 0, 0),
    )
    kept = pl.BlockSpec(
        (1, 1, run, 3 * HALF),
        lambda s, i, order: (jnp.maximum(s, 2) - 2, jnp.where(s < 2, 0, i), 0, 0),
    )
    outs = pl.pallas_call(
        targets_kernel,
        grid_spec=pltpu.PrefetchScalarGridSpec(
            num_scalar_prefetch=1,
            grid=(4, n),
            in_specs=[block_of(dino), block_of(siglip), block_of(sam)],
            out_specs=[kept, sent],
        ),
        out_shape=[jax.ShapeDtypeStruct((2, n, run, 3 * HALF), bf16)] * 2,
        compiler_params=pltpu.CompilerParams(vmem_limit_bytes=12 * MIB),
        cost_estimate=pl.CostEstimate(flops=1000, bytes_accessed=1000, transcendentals=0),
        name="targets",
    )(order, dino, siglip, sam)
    return [o.reshape(2 * n * run, 3 * HALF) for o in outs]


def gelu(x):
    inner = x * (0.7978845608028654 + (0.7978845608028654 * 0.044715) * (x * x))
    half = 0.5 * x
    return half + half * jnp.tanh(inner)


def column_runs(channels):
    return [(n, min(n + 512, channels)) for n in range(0, channels, 512)]


def copies_of(refs, n):
    return refs[:n], refs[n:]


def adapt_kernel(which, fresh, turned, slots, pieces, *refs):
    teachers = len(turned)
    x_in, refs = copies_of(refs, pieces)
    (goal_o_in, goal_s_in), refs = copies_of(refs, 2)
    ins, refs = copies_of(refs, 3 * teachers)
    if not fresh:
        refs = refs[4 * teachers :]
    outs, refs = copies_of(refs, 4 * teachers)
    x, refs = refs[0], refs[1:]
    bufs, refs = copies_of(refs, 6 * teachers)
    in_sem, w1_sem, out_sem = refs
    rows = x.shape[0]
    part = 256
    at_out = pl.ds(which * rows, rows)

    tokens = []
    for i, piece in enumerate(x_in):
        at = sum(p.shape[0] for p in x_in[:i])
        copy = pltpu.make_async_copy(
            piece, x.at[pl.ds(at, piece.shape[0])], in_sem.at[5 * teachers + i]
        )
        tokens.append(copy)
    loads = []
    for t in range(teachers):
        w1_in, w2o_in, w2s_in = ins[3 * t : 3 * t + 3]
        lanes = pl.ds(slots[t] * HALF, HALF)
        w1, w2, goal = bufs[6 * t : 6 * t + 3]
        if turned[t]:
            width = w2o_in.shape[0]
            w2o, w2s = w2.at[pl.ds(0, width)], w2.at[pl.ds(HALF, width)]
        else:
            width = w2o_in.shape[1]
            w2o, w2s = w2.at[:, pl.ds(0, width)], w2.at[:, pl.ds(HALF, width)]
        strips = [
            pltpu.make_async_copy(
                w1_in.at[:, pl.ds(n, to - n)],
                w1.at[:, pl.ds(n, to - n)],
                w1_sem.at[4 * t + i],
            )
            for i, (n, to) in enumerate(column_runs(w1.shape[1]))
        ]
        pairs = (
            (w2o_in, w2o),
            (w2s_in, w2s),
            (goal_o_in.at[at_out, lanes], goal.at[:, pl.ds(0, HALF)]),
            (goal_s_in.at[at_out, lanes], goal.at[:, pl.ds(HALF, HALF)]),
        )
        group = [
            pltpu.make_async_copy(src, dst, in_sem.at[5 * t + i])
            for i, (src, dst) in enumerate(pairs)
        ]
        loads.append((strips, group))
        if turned[t] and width < HALF:
            zeros = jnp.zeros((HALF - width, w2.shape[1]), bf16)
            w2[width:HALF] = zeros
            w2[HALF + width :] = zeros

    queue = tokens + [copy for strips, group in loads for copy in strips + group]
    started = []

    def arrive(copy):
        place = [other is copy for other in queue].index(True)
        while len(started) < min(place + 1 + AHEAD, len(queue)):
            queue[len(started)].start()
            started.append(True)
        copy.wait()

    for copy in tokens:
        arrive(copy)
    stores = []

    def send(t, i):
        copy_from = bufs[6 * t + 2 + i]
        target = outs[4 * t + i]
        target = target.at[:, at_out] if i == 3 else target.at[at_out]
        copy = pltpu.make_async_copy(copy_from, target, out_sem.at[4 * t + i])
        copy.start()
        stores.append(copy)

    for t in range(teachers):
        w1, w2, goal, hidden, pred, sums = bufs[6 * t : 6 * t + 6]
        channels = w1.shape[1]
        strips, group = loads[t]
        for strip, (n, to) in zip(strips, column_runs(channels)):
            arrive(strip)
            for m in range(0, rows, part):
                hidden[m : m + part, n:to] = gelu(
                    jnp.dot(x[m : m + part], w1[:, n:to], preferred_element_type=f32)
                ).astype(bf16)
        send(t, 1)
        for copy in group:
            arrive(copy)
        send(t, 0)
        for m in range(0, rows, part):
            at = slice(m, m + part)
            p = lax.dot_general(
                hidden[at],
                w2[...],
                (((1,), (1 if turned[t] else 0,)), ((), ())),
                preferred_element_type=f32,
            )
            pred[at] = p
            wide = goal[at].astype(f32)
            pred_sq = jnp.sum(p * p, axis=1, keepdims=True)
            goal_sq = jnp.sum(wide * wide, axis=1, keepdims=True)
            cross = jnp.sum(p * wide, axis=1, keepdims=True)
            lane = lax.broadcasted_iota(jnp.int32, (part, 128), 1)
            cols = jnp.where(lane == 0, pred_sq, jnp.where(lane == 1, goal_sq, cross))
            sums[:, at] = jnp.transpose(cols)[:8]
        send(t, 2)
        send(t, 3)
    for copy in stores:
        copy.wait()


def adapt(pieces, which, goals, teachers, slots, prior=None):
    rows, width = sum(p.shape[0] for p in pieces), pieces[0].shape[1]
    turned = tuple(w2o.shape[0] != w1.shape[1] for w1, w2o, *_ in teachers)
    outs, scratch = [], [pltpu.VMEM((rows, width), bf16)]
    for (w1, *_), turn in zip(teachers, turned):
        channels = w1.shape[1]
        wide = 2 * HALF
        outs += [
            jax.ShapeDtypeStruct((2 * rows, wide), bf16),
            jax.ShapeDtypeStruct((2 * rows, channels), bf16),
            jax.ShapeDtypeStruct((2 * rows, wide), f32),
            jax.ShapeDtypeStruct((8, 2 * rows), f32),
        ]
        scratch += [
            pltpu.VMEM(w1.shape, bf16),
            pltpu.VMEM((wide, channels) if turn else (channels, wide), bf16),
            pltpu.VMEM((rows, wide), bf16),
            pltpu.VMEM((rows, channels), bf16),
            pltpu.VMEM((rows, wide), f32),
            pltpu.VMEM((8, rows), f32),
        ]
    n = len(teachers)
    scratch += [
        pltpu.SemaphoreType.DMA((5 * n + len(pieces),)),
        pltpu.SemaphoreType.DMA((4 * n,)),
        pltpu.SemaphoreType.DMA((4 * n,)),
    ]
    args = [*pieces, *goals] + [a for teacher in teachers for a in teacher]
    aliases = {}
    if prior is not None:
        aliases = {len(args) + i: i for i in range(len(outs))}
        args += list(prior)
    anywhere = pl.BlockSpec(memory_space=pl.ANY)
    return pl.pallas_call(
        functools.partial(adapt_kernel, which, prior is None, turned, slots, len(pieces)),
        in_specs=[anywhere] * len(args),
        out_specs=[anywhere] * len(outs),
        out_shape=outs,
        scratch_shapes=scratch,
        input_output_aliases=aliases,
        compiler_params=pltpu.CompilerParams(vmem_limit_bytes=44 * MIB),
        cost_estimate=pl.CostEstimate(flops=1000, bytes_accessed=1000, transcendentals=0),
        name="adapt",
    )(*args)


def strips_of(total, count):
    return [total[:, 128 * i : 128 * (i + 1)] for i in range(count)]


def stacked(parts):
    if len(parts) == 1:
        strips = strips_of(parts[0], 3)
    else:
        m, s = parts
        tail = jnp.concatenate(
            [s[:, 256:], jnp.zeros((m.shape[0] - s.shape[0], 128), f32)], axis=0
        )
        strips = strips_of(m, 2) + [m[:, 256:] + pltpu.roll(tail, 64, 1)] + strips_of(s, 2)
    return jnp.concatenate(strips, axis=0).astype(bf16)


def pack_kernel(order_ref, *refs):
    *ins, send0, send1, keep0, keep1 = refs
    sums = []
    for a, b in zip(ins[::2], ins[1::2]):
        total = a[...].astype(f32) + b[...].astype(f32)
        sums.append(total.reshape(-1, HALF) if total.ndim == 4 else total)
    slot = pl.program_id(0)
    blocks = []
    for j in range(4):
        rows = [total.shape[0] // 4 for total in sums]
        blocks.append(stacked([t[j * r : (j + 1) * r] for t, r in zip(sums, rows)]))
    for i, out in enumerate((send0, send1, keep0, keep1)):

        @pl.when(slot == i)
        def _():
            for j in range(4):
                out[0, order_ref[8 + j]] = blocks[j]


def pack(grads, received, first, later):
    apart = len(grads) == 1
    c = first
    near = [(c ^ 1, 0), (c ^ 2, 0), (c ^ 3, 1), (c ^ 2, 1), (c, 0), (c ^ 3, 0), (c, 1), (c ^ 1, 1)]
    where = [jnp.where(j ^ later == 1, 0, jnp.where(j ^ later == 2, 1, jnp.where(j ^ later == 0, 2, 3))) for j in range(4)]
    if apart:
        block = [p * 4 + place for place, p in near]
    else:
        block = [place * 2 + p for place, p in near]
    order = jnp.stack(block + where).astype(jnp.int32)
    args, specs = [], []
    height = 0
    for grad, other in zip(grads, received):
        rows = grad.shape[0] // 32
        if apart:
            grad, other = [v.reshape(4, 8, rows, v.shape[1]) for v in (grad, other)]
            spec = pl.BlockSpec((4, 1, rows, HALF), lambda s, i, order: (0, order[2 * s + i], 0, 0))
        else:
            spec = pl.BlockSpec((4 * rows, HALF), lambda s, i, order: (order[2 * s + i], 0))
        args += [grad, other]
        specs += [spec] * 2
        height += rows * (3 if apart else (3 if grad is grads[0] else 2))

    def out_spec(slot):
        def place(s, i, order):
            return (jnp.where(s < slot, 0, jnp.where(s > slot, 1, i)), 0, 0, 0)

        return pl.BlockSpec((1, 4, height, 128), place)

    return pl.pallas_call(
        pack_kernel,
        grid_spec=pltpu.PrefetchScalarGridSpec(
            num_scalar_prefetch=1,
            grid=(4, 2),
            in_specs=specs,
            out_specs=[out_spec(slot) for slot in range(4)],
        ),
        out_shape=[jax.ShapeDtypeStruct((2, 4, height, 128), bf16)] * 4,
        compiler_params=pltpu.CompilerParams(vmem_limit_bytes=16 * MIB),
        name="pack",
    )(order, *args)


def exchange(value, axis, mask):
    flip = mask * (8, 4, 1)[axis]
    return lax.ppermute(value.astype(bf16), "dp", [(d, d ^ flip) for d in range(32)]).astype(f32)


def summed(packed, axis):
    later = 2 - axis
    halves = []
    for send, keep, masks in zip(packed[:2], packed[2:], ((1, 3), (3, 1))):
        total = keep.astype(f32) + exchange(send, axis, masks[0])
        halves.append(total[0] + exchange(total[1], axis, masks[1]))
    both = jnp.stack(halves)
    both = both[:, 2:] + exchange(both[:, :2], later, 1)
    return both[:, 0] + exchange(both[:, 1], later, 3)


def unpack(total, rows):
    dino, sam, siglip = rows
    at = 3 * dino
    mixed = total[at + 2 * sam : at + 3 * sam]
    low = at + 3 * sam
    return (
        jnp.concatenate([total[i * dino : (i + 1) * dino] for i in range(3)], axis=1),
        jnp.concatenate(
            [total[low : low + siglip], total[low + siglip : low + 2 * siglip], mixed[:siglip, 64:96]],
            axis=1,
        ),
        jnp.concatenate([total[at : at + sam], total[at + sam : at + 2 * sam], mixed[:, :64]], axis=1),
    )


def shards(
    student,
    dino_feat,
    siglip_feat,
    sam_feat,
    w1_dino,
    w2_dino,
    w1_siglip,
    w2_siglip,
    w1_sam,
    w2_sam,
):
    n_images, row_count, grid, width = student.shape
    n_dp = lax.axis_size("dp")
    g = lax.axis_index("grp")
    total = n_images * n_dp * grid * grid
    own_tokens = n_images * row_count * grid

    own = student.reshape(own_tokens, width)
    cut = own_tokens // 4
    theirs = [lax.ppermute(piece, "grp", CHIP) for piece in (own[:cut], own[cut:])]

    w2s = (w2_dino, jnp.swapaxes(w2_sam, 0, 1), jnp.swapaxes(w2_siglip, 0, 1))
    w2_others = [lax.ppermute(w, "grp", CORE) for w in w2s]

    order = jnp.stack([g ^ 1, g ^ 3, g, g ^ 2]).astype(jnp.int32)
    kept, sent = targets(order, dino_feat, siglip_feat, sam_feat)
    sent, theirs[0], *w2_others = lax.optimization_barrier((sent, theirs[0], *w2_others))
    goals = (kept, lax.ppermute(sent, "grp", CORE))

    teachers = list(zip((w1_dino, w1_sam, w1_siglip), w2s, w2_others))
    firsts = adapt([own], 0, goals, teachers, (0, 1, 2))

    def second(i, to, after=None):
        pieces = list(theirs)
        if after is not None:
            *pieces, after = lax.optimization_barrier((*pieces, after))
        slots = tuple(range(i, to))
        return adapt(pieces, 1, goals, teachers[i:to], slots, firsts[4 * i : 4 * to])

    def gradient(state, after):
        goal, hidden, pred, part = state
        channels = hidden.shape[1]
        scale = channels / math.sqrt(total)
        sums = part + jnp.roll(lax.ppermute(part, "grp", CHIP), own_tokens, axis=1)
        pred_norm = jnp.sqrt(sums[0] + epsilon)
        goal_norm = jnp.sqrt(sums[1] + epsilon)
        product = pred_norm * goal_norm
        on_goal = -scale / product
        on_pred = scale * sums[2] / (product * pred_norm * pred_norm)
        on_goal, on_pred, after = lax.optimization_barrier((on_goal, on_pred, after))
        error = (on_goal[:, None] * goal.astype(f32) + on_pred[:, None] * pred).astype(bf16)
        grad = jnp.einsum("tk,tc->kc", hidden, error, preferred_element_type=f32)
        return grad.astype(bf16)

    dino_state = second(0, 1)
    others = second(1, 3, dino_state[3])
    sam_state, siglip_state = others[:4], others[4:]
    def swap(grad):
        return lax.ppermute(grad[:, HALF:], "grp", CORE)

    index = lax.axis_index("dp")
    x, y, z = index // 8, index // 4 % 2, index % 4
    dino_grad = gradient(dino_state, sam_state[3])
    sam_grad = gradient(sam_state, dino_grad)
    siglip_grad = gradient(siglip_state, sam_grad)
    dino = summed(pack([dino_grad], [swap(dino_grad)], z, x), 2)
    rest = summed(pack([sam_grad, siglip_grad], [swap(sam_grad), swap(siglip_grad)], x, z), 0)
    both = jnp.concatenate([dino, rest], axis=1)
    here, there = jnp.where(y == 0, both[0], both[1]), jnp.where(y == 0, both[1], both[0])
    return unpack(
        here + exchange(there, 1, 1), [w.shape[1] // n_dp for w in (w1_dino, w1_sam, w1_siglip)]
    )


def solution(mesh):
    in_specs = (
        P("dp", "grp", None, None),
        P("dp", None, None, "grp"),
        P("dp", None, None, "grp"),
        P("dp", None, None, "grp"),
        P(),
        P(None, "grp"),
        P(),
        P(None, "grp"),
        P(),
        P(None, "grp"),
    )
    out_specs = (P("dp", "grp"), P("dp", "grp"), P("dp", "grp"))
    return jax.shard_map(shards, mesh=mesh, in_specs=in_specs, out_specs=out_specs, check_vma=False)
```

```python
import functools
import math

import jax
import jax.numpy as jnp
from jax import lax
from jax.experimental import pallas as pl
from jax.experimental.pallas import tpu as pltpu
from jax.sharding import PartitionSpec as P

epsilon = 1e-06

f32 = jnp.float32
bf16 = jnp.bfloat16

CORE = [(g, g ^ 1) for g in range(4)]
CHIP = [(g, g ^ 2) for g in range(4)]

HALF = 384
MIB = 1024 * 1024


def pad_lanes(x):
    rows, width = x.shape
    if width == HALF:
        return x
    return jnp.concatenate([x, jnp.zeros((rows, HALF - width), x.dtype)], axis=1)


def resample_into(out_ref, at, feat_ref):
    _, in_rows, in_cols, width = feat_ref.shape
    out_rows = in_rows * 8 // 9
    slot = lax.broadcasted_iota(jnp.int32, (8, 1), 0).astype(f32)
    right = 0.125 * slot + 0.0625
    for r in range(out_rows):
        weight = 0.125 * (r % 8) + 0.0625
        first = r // 8 * 9 + r % 8
        row = (1.0 - weight) * feat_ref[0, first].astype(f32) + weight * feat_ref[
            0, first + 1
        ].astype(f32)
        blocks = []
        for b in range(in_cols // 9):
            blocks.append(
                (1.0 - right) * row[9 * b : 9 * b + 8] + right * row[9 * b + 1 : 9 * b + 9]
            )
        done = pad_lanes(jnp.concatenate(blocks, axis=0)).astype(bf16)
        count = done.shape[0]
        out_ref[0, 0, r * count : (r + 1) * count, at * HALF : (at + 1) * HALF] = done


def targets_kernel(order_ref, dino, siglip, sam, kept, sent):
    def fill(out):
        resample_into(out, 0, dino)
        resample_into(out, 2, siglip)
        _, rows, cols, width = sam.shape
        out[0, 0, :, HALF : 2 * HALF] = pad_lanes(sam[0].reshape(rows * cols, width))

    slot = pl.program_id(0)

    @pl.when(slot < 2)
    def _():
        fill(sent)

    @pl.when(slot >= 2)
    def _():
        fill(kept)


def targets(order, dino, siglip, sam):
    n = sam.shape[0]
    run = sam.shape[1] // 4 * sam.shape[2]

    def block_of(feat):
        rows = feat.shape[1] // 4
        return pl.BlockSpec(
            (1, rows) + feat.shape[2:], lambda s, i, order: (i, order[s], 0, 0)
        )

    sent = pl.BlockSpec(
        (1, 1, run, 3 * HALF),
        lambda s, i, order: (jnp.minimum(s, 1), jnp.where(s < 2, i, n - 1), 0, 0),
    )
    kept = pl.BlockSpec(
        (1, 1, run, 3 * HALF),
        lambda s, i, order: (jnp.maximum(s, 2) - 2, jnp.where(s < 2, 0, i), 0, 0),
    )
    outs = pl.pallas_call(
        targets_kernel,
        grid_spec=pltpu.PrefetchScalarGridSpec(
            num_scalar_prefetch=1,
            grid=(4, n),
            in_specs=[block_of(dino), block_of(siglip), block_of(sam)],
            out_specs=[kept, sent],
        ),
        out_shape=[jax.ShapeDtypeStruct((2, n, run, 3 * HALF), bf16)] * 2,
        compiler_params=pltpu.CompilerParams(vmem_limit_bytes=12 * MIB),
        cost_estimate=pl.CostEstimate(flops=1000, bytes_accessed=1000, transcendentals=0),
        name="targets",
    )(order, dino, siglip, sam)
    return [o.reshape(2 * n * run, 3 * HALF) for o in outs]


def gelu(x):
    inner = x * (0.7978845608028654 + (0.7978845608028654 * 0.044715) * (x * x))
    half = 0.5 * x
    return half + half * jnp.tanh(inner)


def column_runs(channels):
    return [(n, min(n + 512, channels)) for n in range(0, channels, 512)]


def copies_of(refs, n):
    return refs[:n], refs[n:]


def adapt_kernel(which, fresh, turned, slots, pieces, *refs):
    teachers = len(turned)
    x_in, refs = copies_of(refs, pieces)
    (goal_o_in, goal_s_in), refs = copies_of(refs, 2)
    ins, refs = copies_of(refs, 3 * teachers)
    if not fresh:
        refs = refs[4 * teachers :]
    outs, refs = copies_of(refs, 4 * teachers)
    x, refs = refs[0], refs[1:]
    bufs, refs = copies_of(refs, 6 * teachers)
    in_sem, w1_sem, out_sem = refs
    rows = x.shape[0]
    part = 256
    at_out = pl.ds(which * rows, rows)

    tokens = []
    for i, piece in enumerate(x_in):
        at = sum(p.shape[0] for p in x_in[:i])
        copy = pltpu.make_async_copy(
            piece, x.at[pl.ds(at, piece.shape[0])], in_sem.at[5 * teachers + i]
        )
        copy.start()
        tokens.append(copy)
    loads = []
    for t in range(teachers):
        w1_in, w2o_in, w2s_in = ins[3 * t : 3 * t + 3]
        lanes = pl.ds(slots[t] * HALF, HALF)
        w1, w2, goal = bufs[6 * t : 6 * t + 3]
        if turned[t]:
            width = w2o_in.shape[0]
            w2o, w2s = w2.at[pl.ds(0, width)], w2.at[pl.ds(HALF, width)]
        else:
            width = w2o_in.shape[1]
            w2o, w2s = w2.at[:, pl.ds(0, width)], w2.at[:, pl.ds(HALF, width)]
        strips = [
            pltpu.make_async_copy(
                w1_in.at[:, pl.ds(n, to - n)],
                w1.at[:, pl.ds(n, to - n)],
                w1_sem.at[4 * t + i],
            )
            for i, (n, to) in enumerate(column_runs(w1.shape[1]))
        ]
        pairs = (
            (w2o_in, w2o),
            (w2s_in, w2s),
            (goal_o_in.at[at_out, lanes], goal.at[:, pl.ds(0, HALF)]),
            (goal_s_in.at[at_out, lanes], goal.at[:, pl.ds(HALF, HALF)]),
        )
        group = [
            pltpu.make_async_copy(src, dst, in_sem.at[5 * t + i])
            for i, (src, dst) in enumerate(pairs)
        ]
        for copy in strips + group:
            copy.start()
        loads.append((strips, group))
        if turned[t] and width < HALF:
            zeros = jnp.zeros((HALF - width, w2.shape[1]), bf16)
            w2[width:HALF] = zeros
            w2[HALF + width :] = zeros

    for copy in tokens:
        copy.wait()
    stores = []

    def send(t, i):
        copy_from = bufs[6 * t + 2 + i]
        target = outs[4 * t + i]
        target = target.at[:, at_out] if i == 3 else target.at[at_out]
        copy = pltpu.make_async_copy(copy_from, target, out_sem.at[4 * t + i])
        copy.start()
        stores.append(copy)

    for t in range(teachers):
        w1, w2, goal, hidden, pred, sums = bufs[6 * t : 6 * t + 6]
        channels = w1.shape[1]
        strips, group = loads[t]
        for strip, (n, to) in zip(strips, column_runs(channels)):
            strip.wait()
            for m in range(0, rows, part):
                hidden[m : m + part, n:to] = gelu(
                    jnp.dot(x[m : m + part], w1[:, n:to], preferred_element_type=f32)
                ).astype(bf16)
        send(t, 1)
        for copy in group:
            copy.wait()
        send(t, 0)
        for m in range(0, rows, part):
            at = slice(m, m + part)
            p = lax.dot_general(
                hidden[at],
                w2[...],
                (((1,), (1 if turned[t] else 0,)), ((), ())),
                preferred_element_type=f32,
            )
            pred[at] = p
            wide = goal[at].astype(f32)
            pred_sq = jnp.sum(p * p, axis=1, keepdims=True)
            goal_sq = jnp.sum(wide * wide, axis=1, keepdims=True)
            cross = jnp.sum(p * wide, axis=1, keepdims=True)
            lane = lax.broadcasted_iota(jnp.int32, (part, 128), 1)
            cols = jnp.where(lane == 0, pred_sq, jnp.where(lane == 1, goal_sq, cross))
            sums[:, at] = jnp.transpose(cols)[:8]
        send(t, 2)
        send(t, 3)
    for copy in stores:
        copy.wait()


def adapt(pieces, which, goals, teachers, slots, prior=None):
    rows, width = sum(p.shape[0] for p in pieces), pieces[0].shape[1]
    turned = tuple(w2o.shape[0] != w1.shape[1] for w1, w2o, *_ in teachers)
    outs, scratch = [], [pltpu.VMEM((rows, width), bf16)]
    for (w1, *_), turn in zip(teachers, turned):
        channels = w1.shape[1]
        wide = 2 * HALF
        outs += [
            jax.ShapeDtypeStruct((2 * rows, wide), bf16),
            jax.ShapeDtypeStruct((2 * rows, channels), bf16),
            jax.ShapeDtypeStruct((2 * rows, wide), f32),
            jax.ShapeDtypeStruct((8, 2 * rows), f32),
        ]
        scratch += [
            pltpu.VMEM(w1.shape, bf16),
            pltpu.VMEM((wide, channels) if turn else (channels, wide), bf16),
            pltpu.VMEM((rows, wide), bf16),
            pltpu.VMEM((rows, channels), bf16),
            pltpu.VMEM((rows, wide), f32),
            pltpu.VMEM((8, rows), f32),
        ]
    n = len(teachers)
    scratch += [
        pltpu.SemaphoreType.DMA((5 * n + len(pieces),)),
        pltpu.SemaphoreType.DMA((4 * n,)),
        pltpu.SemaphoreType.DMA((4 * n,)),
    ]
    args = [*pieces, *goals] + [a for teacher in teachers for a in teacher]
    aliases = {}
    if prior is not None:
        aliases = {len(args) + i: i for i in range(len(outs))}
        args += list(prior)
    anywhere = pl.BlockSpec(memory_space=pl.ANY)
    return pl.pallas_call(
        functools.partial(adapt_kernel, which, prior is None, turned, slots, len(pieces)),
        in_specs=[anywhere] * len(args),
        out_specs=[anywhere] * len(outs),
        out_shape=outs,
        scratch_shapes=scratch,
        input_output_aliases=aliases,
        compiler_params=pltpu.CompilerParams(vmem_limit_bytes=44 * MIB),
        cost_estimate=pl.CostEstimate(flops=1000, bytes_accessed=1000, transcendentals=0),
        name="adapt",
    )(*args)


def pack_kernel(blocks, dino, dino_other, sam, sam_other, siglip, siglip_other, out):
    sums = [
        a[...].astype(f32) + b[...].astype(f32)
        for a, b in ((dino, dino_other), (sam, sam_other), (siglip, siglip_other))
    ]
    rows = [total.shape[0] // blocks for total in sums]
    tall = rows[1]
    for j in range(blocks):
        d, m, s = [total[j * r : (j + 1) * r] for total, r in zip(sums, rows)]
        last = jnp.concatenate([s[:, 256:], jnp.zeros((tall - rows[2], 128), f32)], axis=0)
        mixed = m[:, 256:] + pltpu.roll(last, 64, 1)
        strips = [d[:, :128], d[:, 128:256], d[:, 256:], m[:, :128], m[:, 128:256], mixed]
        strips += [s[:, :128], s[:, 128:256]]
        out[j] = jnp.concatenate(strips, axis=0).astype(bf16)


def pack(grads, received, n_dp):
    blocks = 4
    steps = n_dp // blocks
    rows = [g.shape[0] // n_dp for g in grads]
    height = 3 * rows[0] + 3 * rows[1] + 2 * rows[2]
    args, specs = [], []
    for grad, other, r in zip(grads, received, rows):
        args += [grad, other]
        specs += [pl.BlockSpec((r * blocks, HALF), lambda i: (i, 0))] * 2
    return pl.pallas_call(
        functools.partial(pack_kernel, blocks),
        grid=(steps,),
        in_specs=specs,
        out_specs=pl.BlockSpec((blocks, height, 128), lambda i: (i, 0, 0)),
        out_shape=jax.ShapeDtypeStruct((n_dp, height, 128), bf16),
        compiler_params=pltpu.CompilerParams(vmem_limit_bytes=16 * MIB),
        name="pack",
    )(*args)


def unpack_kernel(split, dino, siglip, sam):
    total = split[0].astype(f32)
    for i in range(1, split.shape[0]):
        total += split[i].astype(f32)
    at = 0
    for out, strips in ((dino, 3), (sam, 2)):
        rows = out.shape[0]
        for i in range(strips):
            out[:, 128 * i : 128 * (i + 1)] = total[at : at + rows]
            at += rows
    mixed = total[at : at + sam.shape[0]]
    sam[:, 256:] = mixed[:, : sam.shape[1] - 256]
    siglip[:, 256:] = pltpu.roll(mixed, 64, 1)[: siglip.shape[0], : siglip.shape[1] - 256]
    at += sam.shape[0]
    for i in range(2):
        rows = siglip.shape[0]
        siglip[:, 128 * i : 128 * (i + 1)] = total[at : at + rows]
        at += rows


def unpack(split, shapes):
    return pl.pallas_call(
        unpack_kernel,
        out_shape=[jax.ShapeDtypeStruct(shape, f32) for shape in shapes],
        compiler_params=pltpu.CompilerParams(vmem_limit_bytes=16 * MIB),
        name="unpack",
    )(split)


def shards(
    student,
    dino_feat,
    siglip_feat,
    sam_feat,
    w1_dino,
    w2_dino,
    w1_siglip,
    w2_siglip,
    w1_sam,
    w2_sam,
):
    n_images, row_count, grid, width = student.shape
    n_dp = lax.axis_size("dp")
    g = lax.axis_index("grp")
    total = n_images * n_dp * grid * grid
    own_tokens = n_images * row_count * grid

    own = student.reshape(own_tokens, width)
    cut = own_tokens // 4
    theirs = [lax.ppermute(piece, "grp", CHIP) for piece in (own[:cut], own[cut:])]

    w2s = (w2_dino, jnp.swapaxes(w2_sam, 0, 1), jnp.swapaxes(w2_siglip, 0, 1))
    w2_others = [lax.ppermute(w, "grp", CORE) for w in w2s]

    order = jnp.stack([g ^ 1, g ^ 3, g, g ^ 2]).astype(jnp.int32)
    kept, sent = targets(order, dino_feat, siglip_feat, sam_feat)
    sent, theirs[0], *w2_others = lax.optimization_barrier((sent, theirs[0], *w2_others))
    goals = (kept, lax.ppermute(sent, "grp", CORE))

    teachers = list(zip((w1_dino, w1_sam, w1_siglip), w2s, w2_others))
    firsts = adapt([own], 0, goals, teachers, (0, 1, 2))

    def second(i, to, after=None):
        pieces = list(theirs)
        if after is not None:
            *pieces, after = lax.optimization_barrier((*pieces, after))
        slots = tuple(range(i, to))
        return adapt(pieces, 1, goals, teachers[i:to], slots, firsts[4 * i : 4 * to])

    def gradient(state, after):
        goal, hidden, pred, part = state
        channels = hidden.shape[1]
        scale = channels / math.sqrt(total)
        sums = part + jnp.roll(lax.ppermute(part, "grp", CHIP), own_tokens, axis=1)
        pred_norm = jnp.sqrt(sums[0] + epsilon)
        goal_norm = jnp.sqrt(sums[1] + epsilon)
        product = pred_norm * goal_norm
        on_goal = -scale / product
        on_pred = scale * sums[2] / (product * pred_norm * pred_norm)
        on_goal, on_pred, after = lax.optimization_barrier((on_goal, on_pred, after))
        error = (on_goal[:, None] * goal.astype(f32) + on_pred[:, None] * pred).astype(bf16)
        grad = jnp.einsum("tk,tc->kc", hidden, error, preferred_element_type=f32)
        return grad.astype(bf16)

    dino_state = second(0, 1)
    others = second(1, 3, dino_state[3])
    sam_state, siglip_state = others[:4], others[4:]
    grads = [gradient(dino_state, sam_state[3])]
    grads.append(gradient(sam_state, grads[0]))
    grads.append(gradient(siglip_state, grads[1]))
    received = [lax.ppermute(grad[:, HALF:], "grp", CORE) for grad in grads]
    split = lax.all_to_all(pack(grads, received, n_dp), "dp", 0, 0, tiled=True)
    shapes = [(w.shape[0] // n_dp, w.shape[1]) for w in (w2_dino, w2_siglip, w2_sam)]
    return tuple(unpack(split, shapes))


def solution(mesh):
    in_specs = (
        P("dp", "grp", None, None),
        P("dp", None, None, "grp"),
        P("dp", None, None, "grp"),
        P("dp", None, None, "grp"),
        P(),
        P(None, "grp"),
        P(),
        P(None, "grp"),
        P(),
        P(None, "grp"),
    )
    out_specs = (P("dp", "grp"), P("dp", "grp"), P("dp", "grp"))
    return jax.shard_map(shards, mesh=mesh, in_specs=in_specs, out_specs=out_specs, check_vma=False)
```

```python
import functools
import math

import jax
import jax.numpy as jnp
from jax import lax
from jax.experimental import pallas as pl
from jax.experimental.pallas import tpu as pltpu
from jax.sharding import PartitionSpec as P

epsilon = 1e-06

f32 = jnp.float32
bf16 = jnp.bfloat16

CORE = [(g, g ^ 1) for g in range(4)]
CHIP = [(g, g ^ 2) for g in range(4)]

HALF = 384
MIB = 1024 * 1024


def pad_lanes(x):
    rows, width = x.shape
    if width == HALF:
        return x
    return jnp.concatenate([x, jnp.zeros((rows, HALF - width), x.dtype)], axis=1)


def resample_into(out_ref, at, feat_ref):
    _, in_rows, in_cols, width = feat_ref.shape
    out_rows = in_rows * 8 // 9
    slot = lax.broadcasted_iota(jnp.int32, (8, 1), 0).astype(f32)
    right = 0.125 * slot + 0.0625
    for r in range(out_rows):
        weight = 0.125 * (r % 8) + 0.0625
        first = r // 8 * 9 + r % 8
        row = (1.0 - weight) * feat_ref[0, first].astype(f32) + weight * feat_ref[
            0, first + 1
        ].astype(f32)
        blocks = []
        for b in range(in_cols // 9):
            blocks.append(
                (1.0 - right) * row[9 * b : 9 * b + 8] + right * row[9 * b + 1 : 9 * b + 9]
            )
        done = pad_lanes(jnp.concatenate(blocks, axis=0)).astype(bf16)
        count = done.shape[0]
        out_ref[0, 0, r * count : (r + 1) * count, at * HALF : (at + 1) * HALF] = done


def targets_kernel(order_ref, dino, siglip, sam, kept, sent):
    def fill(out):
        resample_into(out, 0, dino)
        resample_into(out, 2, siglip)
        _, rows, cols, width = sam.shape
        out[0, 0, :, HALF : 2 * HALF] = pad_lanes(sam[0].reshape(rows * cols, width))

    slot = pl.program_id(0)

    @pl.when(slot < 2)
    def _():
        fill(sent)

    @pl.when(slot >= 2)
    def _():
        fill(kept)


def targets(order, dino, siglip, sam):
    n = sam.shape[0]
    run = sam.shape[1] // 4 * sam.shape[2]

    def block_of(feat):
        rows = feat.shape[1] // 4
        return pl.BlockSpec(
            (1, rows) + feat.shape[2:], lambda s, i, order: (i, order[s], 0, 0)
        )

    sent = pl.BlockSpec(
        (1, 1, run, 3 * HALF),
        lambda s, i, order: (jnp.minimum(s, 1), jnp.where(s < 2, i, n - 1), 0, 0),
    )
    kept = pl.BlockSpec(
        (1, 1, run, 3 * HALF),
        lambda s, i, order: (jnp.maximum(s, 2) - 2, jnp.where(s < 2, 0, i), 0, 0),
    )
    outs = pl.pallas_call(
        targets_kernel,
        grid_spec=pltpu.PrefetchScalarGridSpec(
            num_scalar_prefetch=1,
            grid=(4, n),
            in_specs=[block_of(dino), block_of(siglip), block_of(sam)],
            out_specs=[kept, sent],
        ),
        out_shape=[jax.ShapeDtypeStruct((2, n, run, 3 * HALF), bf16)] * 2,
        compiler_params=pltpu.CompilerParams(vmem_limit_bytes=12 * MIB),
        cost_estimate=pl.CostEstimate(flops=1000, bytes_accessed=1000, transcendentals=0),
        name="targets",
    )(order, dino, siglip, sam)
    return [o.reshape(2 * n * run, 3 * HALF) for o in outs]


def gelu(x):
    inner = x * (0.7978845608028654 + (0.7978845608028654 * 0.044715) * (x * x))
    half = 0.5 * x
    return half + half * jnp.tanh(inner)


def column_runs(channels):
    return [(n, min(n + 512, channels)) for n in range(0, channels, 512)]


def copies_of(refs, n):
    return refs[:n], refs[n:]


def adapt_kernel(which, fresh, turned, slots, pieces, *refs):
    teachers = len(turned)
    x_in, refs = copies_of(refs, pieces)
    goals_in, refs = copies_of(refs, 2 if fresh else teachers)
    ins, refs = copies_of(refs, 3 * teachers)
    if not fresh:
        refs = refs[3 * teachers :]
    outs, refs = copies_of(refs, (4 if fresh else 3) * teachers)
    x, refs = refs[0], refs[1:]
    bufs, refs = copies_of(refs, 6 * teachers)
    in_sem, w1_sem, out_sem = refs
    rows = x.shape[0]
    part = 256
    at_out = pl.ds(which * rows, rows)

    tokens = []
    for i, piece in enumerate(x_in):
        at = sum(p.shape[0] for p in x_in[:i])
        copy = pltpu.make_async_copy(
            piece, x.at[pl.ds(at, piece.shape[0])], in_sem.at[5 * teachers + i]
        )
        copy.start()
        tokens.append(copy)
    loads = []
    for t in range(teachers):
        w1_in, w2o_in, w2s_in = ins[3 * t : 3 * t + 3]
        lanes = pl.ds(slots[t] * HALF, HALF)
        w1, w2, goal = bufs[6 * t : 6 * t + 3]
        if turned[t]:
            width = w2o_in.shape[0]
            w2o, w2s = w2.at[pl.ds(0, width)], w2.at[pl.ds(HALF, width)]
        else:
            width = w2o_in.shape[1]
            w2o, w2s = w2.at[:, pl.ds(0, width)], w2.at[:, pl.ds(HALF, width)]
        strips = [
            pltpu.make_async_copy(
                w1_in.at[:, pl.ds(n, to - n)],
                w1.at[:, pl.ds(n, to - n)],
                w1_sem.at[4 * t + i],
            )
            for i, (n, to) in enumerate(column_runs(w1.shape[1]))
        ]
        pairs = (
            (w2o_in, w2o),
            (w2s_in, w2s),
        )
        if fresh:
            pairs += tuple(
                (side.at[at_out, lanes], goal.at[:, pl.ds(i * HALF, HALF)])
                for i, side in enumerate(goals_in)
            )
        else:
            pairs += ((goals_in[t].at[at_out], goal),)
        group = [
            pltpu.make_async_copy(src, dst, in_sem.at[5 * t + i])
            for i, (src, dst) in enumerate(pairs)
        ]
        for copy in strips + group:
            copy.start()
        loads.append((strips, group))
        if turned[t] and width < HALF:
            zeros = jnp.zeros((HALF - width, w2.shape[1]), bf16)
            w2[width:HALF] = zeros
            w2[HALF + width :] = zeros

    for copy in tokens:
        copy.wait()
    stores = []
    if fresh:
        later = pl.ds(rows, rows)
        for t in range(teachers):
            for i, side in enumerate(goals_in):
                copy = pltpu.make_async_copy(
                    side.at[later, pl.ds(slots[t] * HALF, HALF)],
                    outs[4 * t].at[later, pl.ds(i * HALF, HALF)],
                    out_sem.at[4 * teachers + 2 * t + i],
                )
                copy.start()
                stores.append(copy)

    def send(t, i):
        copy_from = bufs[6 * t + 2 + i]
        if i == 0 and not fresh:
            return
        target = outs[4 * t + i if fresh else 3 * t + i - 1]
        target = target.at[:, at_out] if i == 3 else target.at[at_out]
        copy = pltpu.make_async_copy(copy_from, target, out_sem.at[4 * t + i])
        copy.start()
        stores.append(copy)

    for t in range(teachers):
        w1, w2, goal, hidden, pred, sums = bufs[6 * t : 6 * t + 6]
        channels = w1.shape[1]
        strips, group = loads[t]
        for strip, (n, to) in zip(strips, column_runs(channels)):
            strip.wait()
            for m in range(0, rows, part):
                hidden[m : m + part, n:to] = gelu(
                    jnp.dot(x[m : m + part], w1[:, n:to], preferred_element_type=f32)
                ).astype(bf16)
        send(t, 1)
        for copy in group:
            copy.wait()
        send(t, 0)
        for m in range(0, rows, part):
            at = slice(m, m + part)
            p = lax.dot_general(
                hidden[at],
                w2[...],
                (((1,), (1 if turned[t] else 0,)), ((), ())),
                preferred_element_type=f32,
            )
            pred[at] = p
            wide = goal[at].astype(f32)
            pred_sq = jnp.sum(p * p, axis=1, keepdims=True)
            goal_sq = jnp.sum(wide * wide, axis=1, keepdims=True)
            cross = jnp.sum(p * wide, axis=1, keepdims=True)
            lane = lax.broadcasted_iota(jnp.int32, (part, 128), 1)
            cols = jnp.where(lane == 0, pred_sq, jnp.where(lane == 1, goal_sq, cross))
            sums[:, at] = jnp.transpose(cols)[:8]
        send(t, 2)
        send(t, 3)
    for copy in stores:
        copy.wait()


def adapt(pieces, which, goals, teachers, slots, prior=None):
    rows, width = sum(p.shape[0] for p in pieces), pieces[0].shape[1]
    turned = tuple(w2o.shape[0] != w1.shape[1] for w1, w2o, *_ in teachers)
    outs, scratch = [], [pltpu.VMEM((rows, width), bf16)]
    for (w1, *_), turn in zip(teachers, turned):
        channels = w1.shape[1]
        wide = 2 * HALF
        if prior is None:
            outs.append(jax.ShapeDtypeStruct((2 * rows, wide), bf16))
        outs += [
            jax.ShapeDtypeStruct((2 * rows, channels), bf16),
            jax.ShapeDtypeStruct((2 * rows, wide), f32),
            jax.ShapeDtypeStruct((8, 2 * rows), f32),
        ]
        scratch += [
            pltpu.VMEM(w1.shape, bf16),
            pltpu.VMEM((wide, channels) if turn else (channels, wide), bf16),
            pltpu.VMEM((rows, wide), bf16),
            pltpu.VMEM((rows, channels), bf16),
            pltpu.VMEM((rows, wide), f32),
            pltpu.VMEM((8, rows), f32),
        ]
    n = len(teachers)
    scratch += [
        pltpu.SemaphoreType.DMA((5 * n + len(pieces),)),
        pltpu.SemaphoreType.DMA((4 * n,)),
        pltpu.SemaphoreType.DMA((6 * n,)),
    ]
    args = [*pieces, *goals] + [a for teacher in teachers for a in teacher]
    aliases = {}
    if prior is not None:
        aliases = {len(args) + i: i for i in range(len(outs))}
        args += list(prior)
    anywhere = pl.BlockSpec(memory_space=pl.ANY)
    return pl.pallas_call(
        functools.partial(adapt_kernel, which, prior is None, turned, slots, len(pieces)),
        in_specs=[anywhere] * len(args),
        out_specs=[anywhere] * len(outs),
        out_shape=outs,
        scratch_shapes=scratch,
        input_output_aliases=aliases,
        compiler_params=pltpu.CompilerParams(vmem_limit_bytes=44 * MIB),
        cost_estimate=pl.CostEstimate(flops=1000, bytes_accessed=1000, transcendentals=0),
        name="adapt",
    )(*args)


def pack_kernel(blocks, dino, dino_other, sam, sam_other, siglip, siglip_other, out):
    sums = [
        a[...].astype(f32) + b[...].astype(f32)
        for a, b in ((dino, dino_other), (sam, sam_other), (siglip, siglip_other))
    ]
    rows = [total.shape[0] // blocks for total in sums]
    tall = rows[1]
    for j in range(blocks):
        d, m, s = [total[j * r : (j + 1) * r] for total, r in zip(sums, rows)]
        last = jnp.concatenate([s[:, 256:], jnp.zeros((tall - rows[2], 128), f32)], axis=0)
        mixed = m[:, 256:] + pltpu.roll(last, 64, 1)
        strips = [d[:, :128], d[:, 128:256], d[:, 256:], m[:, :128], m[:, 128:256], mixed]
        strips += [s[:, :128], s[:, 128:256]]
        out[j] = jnp.concatenate(strips, axis=0).astype(bf16)


def pack(grads, received, n_dp):
    blocks = 4
    steps = n_dp // blocks
    rows = [g.shape[0] // n_dp for g in grads]
    height = 3 * rows[0] + 3 * rows[1] + 2 * rows[2]
    args, specs = [], []
    for grad, other, r in zip(grads, received, rows):
        args += [grad, other]
        specs += [pl.BlockSpec((r * blocks, HALF), lambda i: (i, 0))] * 2
    return pl.pallas_call(
        functools.partial(pack_kernel, blocks),
        grid=(steps,),
        in_specs=specs,
        out_specs=pl.BlockSpec((blocks, height, 128), lambda i: (i, 0, 0)),
        out_shape=jax.ShapeDtypeStruct((n_dp, height, 128), bf16),
        compiler_params=pltpu.CompilerParams(vmem_limit_bytes=16 * MIB),
        name="pack",
    )(*args)


def unpack_kernel(split, dino, siglip, sam):
    total = split[0].astype(f32)
    for i in range(1, split.shape[0]):
        total += split[i].astype(f32)
    at = 0
    for out, strips in ((dino, 3), (sam, 2)):
        rows = out.shape[0]
        for i in range(strips):
            out[:, 128 * i : 128 * (i + 1)] = total[at : at + rows]
            at += rows
    mixed = total[at : at + sam.shape[0]]
    sam[:, 256:] = mixed[:, : sam.shape[1] - 256]
    siglip[:, 256:] = pltpu.roll(mixed, 64, 1)[: siglip.shape[0], : siglip.shape[1] - 256]
    at += sam.shape[0]
    for i in range(2):
        rows = siglip.shape[0]
        siglip[:, 128 * i : 128 * (i + 1)] = total[at : at + rows]
        at += rows


def unpack(split, shapes):
    return pl.pallas_call(
        unpack_kernel,
        out_shape=[jax.ShapeDtypeStruct(shape, f32) for shape in shapes],
        compiler_params=pltpu.CompilerParams(vmem_limit_bytes=16 * MIB),
        name="unpack",
    )(split)


def shards(
    student,
    dino_feat,
    siglip_feat,
    sam_feat,
    w1_dino,
    w2_dino,
    w1_siglip,
    w2_siglip,
    w1_sam,
    w2_sam,
):
    n_images, row_count, grid, width = student.shape
    n_dp = lax.axis_size("dp")
    g = lax.axis_index("grp")
    total = n_images * n_dp * grid * grid
    own_tokens = n_images * row_count * grid

    own = student.reshape(own_tokens, width)
    cut = own_tokens // 4
    theirs = [lax.ppermute(piece, "grp", CHIP) for piece in (own[:cut], own[cut:])]

    w2s = (w2_dino, jnp.swapaxes(w2_sam, 0, 1), jnp.swapaxes(w2_siglip, 0, 1))
    w2_others = [lax.ppermute(w, "grp", CORE) for w in w2s]

    order = jnp.stack([g ^ 1, g ^ 3, g, g ^ 2]).astype(jnp.int32)
    kept, sent = targets(order, dino_feat, siglip_feat, sam_feat)
    sent, theirs[0], *w2_others = lax.optimization_barrier((sent, theirs[0], *w2_others))
    goals = (kept, lax.ppermute(sent, "grp", CORE))

    teachers = list(zip((w1_dino, w1_sam, w1_siglip), w2s, w2_others))
    firsts = adapt([own], 0, goals, teachers, (0, 1, 2))

    def second(i, to, after=None):
        pieces = list(theirs)
        if after is not None:
            *pieces, after = lax.optimization_barrier((*pieces, after))
        slots = tuple(range(i, to))
        held = [firsts[4 * t : 4 * t + 4] for t in slots]
        results = adapt(
            pieces, 1, [h[0] for h in held], teachers[i:to], slots, [r for h in held for r in h[1:]]
        )
        return [r for k, h in enumerate(held) for r in (h[0], *results[3 * k : 3 * k + 3])]

    def gradient(state, after):
        goal, hidden, pred, part = state
        channels = hidden.shape[1]
        scale = channels / math.sqrt(total)
        sums = part + jnp.roll(lax.ppermute(part, "grp", CHIP), own_tokens, axis=1)
        pred_norm = jnp.sqrt(sums[0] + epsilon)
        goal_norm = jnp.sqrt(sums[1] + epsilon)
        product = pred_norm * goal_norm
        on_goal = -scale / product
        on_pred = scale * sums[2] / (product * pred_norm * pred_norm)
        on_goal, on_pred, after = lax.optimization_barrier((on_goal, on_pred, after))
        error = (on_goal[:, None] * goal.astype(f32) + on_pred[:, None] * pred).astype(bf16)
        grad = jnp.einsum("tk,tc->kc", hidden, error, preferred_element_type=f32)
        return grad.astype(bf16)

    dino_state = second(0, 1)
    others = second(1, 3, dino_state[3])
    sam_state, siglip_state = others[:4], others[4:]
    grads = [gradient(dino_state, sam_state[3])]
    grads.append(gradient(sam_state, grads[0]))
    grads.append(gradient(siglip_state, grads[1]))
    received = [lax.ppermute(grad[:, HALF:], "grp", CORE) for grad in grads]
    split = lax.all_to_all(pack(grads, received, n_dp), "dp", 0, 0, tiled=True)
    shapes = [(w.shape[0] // n_dp, w.shape[1]) for w in (w2_dino, w2_siglip, w2_sam)]
    return tuple(unpack(split, shapes))


def solution(mesh):
    in_specs = (
        P("dp", "grp", None, None),
        P("dp", None, None, "grp"),
        P("dp", None, None, "grp"),
        P("dp", None, None, "grp"),
        P(),
        P(None, "grp"),
        P(),
        P(None, "grp"),
        P(),
        P(None, "grp"),
    )
    out_specs = (P("dp", "grp"), P("dp", "grp"), P("dp", "grp"))
    return jax.shard_map(shards, mesh=mesh, in_specs=in_specs, out_specs=out_specs, check_vma=False)
```

```python
import functools
import math

import jax
import jax.numpy as jnp
from jax import lax
from jax.experimental import pallas as pl
from jax.experimental.pallas import tpu as pltpu
from jax.sharding import PartitionSpec as P

epsilon = 1e-06

f32 = jnp.float32
bf16 = jnp.bfloat16

CORE = [(g, g ^ 1) for g in range(4)]
CHIP = [(g, g ^ 2) for g in range(4)]

HALF = 384
MIB = 1024 * 1024


def pad_lanes(x):
    rows, width = x.shape
    if width == HALF:
        return x
    return jnp.concatenate([x, jnp.zeros((rows, HALF - width), x.dtype)], axis=1)


def resample_into(out_ref, at, feat_ref):
    _, in_rows, in_cols, width = feat_ref.shape
    out_rows = in_rows * 8 // 9
    slot = lax.broadcasted_iota(jnp.int32, (8, 1), 0).astype(f32)
    right = 0.125 * slot + 0.0625
    for r in range(out_rows):
        weight = 0.125 * (r % 8) + 0.0625
        first = r // 8 * 9 + r % 8
        row = (1.0 - weight) * feat_ref[0, first].astype(f32) + weight * feat_ref[
            0, first + 1
        ].astype(f32)
        blocks = []
        for b in range(in_cols // 9):
            blocks.append(
                (1.0 - right) * row[9 * b : 9 * b + 8] + right * row[9 * b + 1 : 9 * b + 9]
            )
        done = pad_lanes(jnp.concatenate(blocks, axis=0)).astype(bf16)
        count = done.shape[0]
        out_ref[0, 0, r * count : (r + 1) * count, at * HALF : (at + 1) * HALF] = done


def targets_kernel(order_ref, dino, siglip, sam, kept, sent):
    def fill(out):
        resample_into(out, 0, dino)
        resample_into(out, 2, siglip)
        _, rows, cols, width = sam.shape
        out[0, 0, :, HALF : 2 * HALF] = pad_lanes(sam[0].reshape(rows * cols, width))

    slot = pl.program_id(0)

    @pl.when(slot < 2)
    def _():
        fill(sent)

    @pl.when(slot >= 2)
    def _():
        fill(kept)


def targets(order, dino, siglip, sam):
    n = sam.shape[0]
    run = sam.shape[1] // 4 * sam.shape[2]

    def block_of(feat):
        rows = feat.shape[1] // 4
        return pl.BlockSpec(
            (1, rows) + feat.shape[2:], lambda s, i, order: (i, order[s], 0, 0)
        )

    sent = pl.BlockSpec(
        (1, 1, run, 3 * HALF),
        lambda s, i, order: (jnp.minimum(s, 1), jnp.where(s < 2, i, n - 1), 0, 0),
    )
    kept = pl.BlockSpec(
        (1, 1, run, 3 * HALF),
        lambda s, i, order: (jnp.maximum(s, 2) - 2, jnp.where(s < 2, 0, i), 0, 0),
    )
    outs = pl.pallas_call(
        targets_kernel,
        grid_spec=pltpu.PrefetchScalarGridSpec(
            num_scalar_prefetch=1,
            grid=(4, n),
            in_specs=[block_of(dino), block_of(siglip), block_of(sam)],
            out_specs=[kept, sent],
        ),
        out_shape=[jax.ShapeDtypeStruct((2, n, run, 3 * HALF), bf16)] * 2,
        compiler_params=pltpu.CompilerParams(vmem_limit_bytes=12 * MIB),
        cost_estimate=pl.CostEstimate(flops=1000, bytes_accessed=1000, transcendentals=0),
        name="targets",
    )(order, dino, siglip, sam)
    return [o.reshape(2 * n * run, 3 * HALF) for o in outs]


def gelu(x):
    inner = x * (0.7978845608028654 + (0.7978845608028654 * 0.044715) * (x * x))
    half = 0.5 * x
    return half + half * jnp.tanh(inner)


def column_runs(channels):
    return [(n, min(n + 512, channels)) for n in range(0, channels, 512)]


def copies_of(refs, n):
    return refs[:n], refs[n:]


def adapt_kernel(which, fresh, turned, slots, pieces, *refs):
    teachers = len(turned)
    x_in, refs = copies_of(refs, pieces)
    (goal_o_in, goal_s_in), refs = copies_of(refs, 2)
    ins, refs = copies_of(refs, 3 * teachers)
    if not fresh:
        refs = refs[4 * teachers :]
    outs, refs = copies_of(refs, 4 * teachers)
    x, refs = refs[0], refs[1:]
    bufs, refs = copies_of(refs, 6 * teachers)
    in_sem, w1_sem, out_sem = refs
    rows = x.shape[0]
    part = 256
    at_out = pl.ds(which * rows, rows)

    tokens = []
    for i, piece in enumerate(x_in):
        at = sum(p.shape[0] for p in x_in[:i])
        copy = pltpu.make_async_copy(
            piece, x.at[pl.ds(at, piece.shape[0])], in_sem.at[5 * teachers + i]
        )
        copy.start()
        tokens.append(copy)
    loads = []
    for t in range(teachers):
        w1_in, w2o_in, w2s_in = ins[3 * t : 3 * t + 3]
        lanes = pl.ds(slots[t] * HALF, HALF)
        w1, w2, goal = bufs[6 * t : 6 * t + 3]
        if turned[t]:
            width = w2o_in.shape[0]
            w2o, w2s = w2.at[pl.ds(0, width)], w2.at[pl.ds(HALF, width)]
        else:
            width = w2o_in.shape[1]
            w2o, w2s = w2.at[:, pl.ds(0, width)], w2.at[:, pl.ds(HALF, width)]
        strips = [
            pltpu.make_async_copy(
                w1_in.at[:, pl.ds(n, to - n)],
                w1.at[:, pl.ds(n, to - n)],
                w1_sem.at[4 * t + i],
            )
            for i, (n, to) in enumerate(column_runs(w1.shape[1]))
        ]
        pairs = (
            (w2o_in, w2o),
            (w2s_in, w2s),
            (goal_o_in.at[at_out, lanes], goal.at[:, pl.ds(0, HALF)]),
            (goal_s_in.at[at_out, lanes], goal.at[:, pl.ds(HALF, HALF)]),
        )
        group = [
            pltpu.make_async_copy(src, dst, in_sem.at[5 * t + i])
            for i, (src, dst) in enumerate(pairs)
        ]
        for copy in strips + group:
            copy.start()
        loads.append((strips, group))
        if turned[t] and width < HALF:
            zeros = jnp.zeros((HALF - width, w2.shape[1]), bf16)
            w2[width:HALF] = zeros
            w2[HALF + width :] = zeros

    for copy in tokens:
        copy.wait()
    stores = []

    def send(t, i):
        copy_from = bufs[6 * t + 2 + i]
        target = outs[4 * t + i]
        target = target.at[:, at_out] if i == 3 else target.at[at_out]
        copy = pltpu.make_async_copy(copy_from, target, out_sem.at[4 * t + i])
        copy.start()
        stores.append(copy)

    for t in range(teachers):
        w1, w2, goal, hidden, pred, sums = bufs[6 * t : 6 * t + 6]
        channels = w1.shape[1]
        strips, group = loads[t]
        for strip, (n, to) in zip(strips, column_runs(channels)):
            strip.wait()
            for m in range(0, rows, part):
                hidden[m : m + part, n:to] = gelu(
                    jnp.dot(x[m : m + part], w1[:, n:to], preferred_element_type=f32)
                ).astype(bf16)
        send(t, 1)
        for copy in group:
            copy.wait()
        send(t, 0)
        for m in range(0, rows, part):
            at = slice(m, m + part)
            p = lax.dot_general(
                hidden[at],
                w2[...],
                (((1,), (1 if turned[t] else 0,)), ((), ())),
                preferred_element_type=f32,
            )
            pred[at] = p
            wide = goal[at].astype(f32)
            pred_sq = jnp.sum(p * p, axis=1, keepdims=True)
            goal_sq = jnp.sum(wide * wide, axis=1, keepdims=True)
            cross = jnp.sum(p * wide, axis=1, keepdims=True)
            lane = lax.broadcasted_iota(jnp.int32, (part, 128), 1)
            cols = jnp.where(lane == 0, pred_sq, jnp.where(lane == 1, goal_sq, cross))
            sums[:, at] = jnp.transpose(cols)[:8]
        send(t, 2)
        send(t, 3)
    for copy in stores:
        copy.wait()


def adapt(pieces, which, goals, teachers, slots, prior=None):
    rows, width = sum(p.shape[0] for p in pieces), pieces[0].shape[1]
    turned = tuple(w2o.shape[0] != w1.shape[1] for w1, w2o, *_ in teachers)
    outs, scratch = [], [pltpu.VMEM((rows, width), bf16)]
    for (w1, *_), turn in zip(teachers, turned):
        channels = w1.shape[1]
        wide = 2 * HALF
        outs += [
            jax.ShapeDtypeStruct((2 * rows, wide), bf16),
            jax.ShapeDtypeStruct((2 * rows, channels), bf16),
            jax.ShapeDtypeStruct((2 * rows, wide), f32),
            jax.ShapeDtypeStruct((8, 2 * rows), f32),
        ]
        scratch += [
            pltpu.VMEM(w1.shape, bf16),
            pltpu.VMEM((wide, channels) if turn else (channels, wide), bf16),
            pltpu.VMEM((rows, wide), bf16),
            pltpu.VMEM((rows, channels), bf16),
            pltpu.VMEM((rows, wide), f32),
            pltpu.VMEM((8, rows), f32),
        ]
    n = len(teachers)
    scratch += [
        pltpu.SemaphoreType.DMA((5 * n + len(pieces),)),
        pltpu.SemaphoreType.DMA((4 * n,)),
        pltpu.SemaphoreType.DMA((4 * n,)),
    ]
    args = [*pieces, *goals] + [a for teacher in teachers for a in teacher]
    aliases = {}
    if prior is not None:
        aliases = {len(args) + i: i for i in range(len(outs))}
        args += list(prior)
    anywhere = pl.BlockSpec(memory_space=pl.ANY)
    return pl.pallas_call(
        functools.partial(adapt_kernel, which, prior is None, turned, slots, len(pieces)),
        in_specs=[anywhere] * len(args),
        out_specs=[anywhere] * len(outs),
        out_shape=outs,
        scratch_shapes=scratch,
        input_output_aliases=aliases,
        compiler_params=pltpu.CompilerParams(vmem_limit_bytes={1: 61, 2: 50, 3: 44}[n] * MIB),
        cost_estimate=pl.CostEstimate(flops=1000, bytes_accessed=1000, transcendentals=0),
        name="adapt",
    )(*args)


def pack_kernel(blocks, dino, dino_other, sam, sam_other, siglip, siglip_other, out):
    sums = [
        a[...].astype(f32) + b[...].astype(f32)
        for a, b in ((dino, dino_other), (sam, sam_other), (siglip, siglip_other))
    ]
    rows = [total.shape[0] // blocks for total in sums]
    tall = rows[1]
    for j in range(blocks):
        d, m, s = [total[j * r : (j + 1) * r] for total, r in zip(sums, rows)]
        last = jnp.concatenate([s[:, 256:], jnp.zeros((tall - rows[2], 128), f32)], axis=0)
        mixed = m[:, 256:] + pltpu.roll(last, 64, 1)
        strips = [d[:, :128], d[:, 128:256], d[:, 256:], m[:, :128], m[:, 128:256], mixed]
        strips += [s[:, :128], s[:, 128:256]]
        out[j] = jnp.concatenate(strips, axis=0).astype(bf16)


def pack(grads, received, n_dp):
    blocks = 4
    steps = n_dp // blocks
    rows = [g.shape[0] // n_dp for g in grads]
    height = 3 * rows[0] + 3 * rows[1] + 2 * rows[2]
    args, specs = [], []
    for grad, other, r in zip(grads, received, rows):
        args += [grad, other]
        specs += [pl.BlockSpec((r * blocks, HALF), lambda i: (i, 0))] * 2
    return pl.pallas_call(
        functools.partial(pack_kernel, blocks),
        grid=(steps,),
        in_specs=specs,
        out_specs=pl.BlockSpec((blocks, height, 128), lambda i: (i, 0, 0)),
        out_shape=jax.ShapeDtypeStruct((n_dp, height, 128), bf16),
        compiler_params=pltpu.CompilerParams(vmem_limit_bytes=16 * MIB),
        name="pack",
    )(*args)


def unpack_kernel(split, dino, siglip, sam):
    total = split[0].astype(f32)
    for i in range(1, split.shape[0]):
        total += split[i].astype(f32)
    at = 0
    for out, strips in ((dino, 3), (sam, 2)):
        rows = out.shape[0]
        for i in range(strips):
            out[:, 128 * i : 128 * (i + 1)] = total[at : at + rows]
            at += rows
    mixed = total[at : at + sam.shape[0]]
    sam[:, 256:] = mixed[:, : sam.shape[1] - 256]
    siglip[:, 256:] = pltpu.roll(mixed, 64, 1)[: siglip.shape[0], : siglip.shape[1] - 256]
    at += sam.shape[0]
    for i in range(2):
        rows = siglip.shape[0]
        siglip[:, 128 * i : 128 * (i + 1)] = total[at : at + rows]
        at += rows


def unpack(split, shapes):
    return pl.pallas_call(
        unpack_kernel,
        out_shape=[jax.ShapeDtypeStruct(shape, f32) for shape in shapes],
        compiler_params=pltpu.CompilerParams(vmem_limit_bytes=16 * MIB),
        name="unpack",
    )(split)


def shards(
    student,
    dino_feat,
    siglip_feat,
    sam_feat,
    w1_dino,
    w2_dino,
    w1_siglip,
    w2_siglip,
    w1_sam,
    w2_sam,
):
    n_images, row_count, grid, width = student.shape
    n_dp = lax.axis_size("dp")
    g = lax.axis_index("grp")
    total = n_images * n_dp * grid * grid
    own_tokens = n_images * row_count * grid

    own = student.reshape(own_tokens, width)
    cut = own_tokens // 4
    theirs = [lax.ppermute(piece, "grp", CHIP) for piece in (own[:cut], own[cut:])]

    w2s = (w2_dino, jnp.swapaxes(w2_sam, 0, 1), jnp.swapaxes(w2_siglip, 0, 1))
    w2_others = [lax.ppermute(w, "grp", CORE) for w in w2s]

    order = jnp.stack([g ^ 1, g ^ 3, g, g ^ 2]).astype(jnp.int32)
    kept, sent = targets(order, dino_feat, siglip_feat, sam_feat)
    sent, theirs[0], *w2_others = lax.optimization_barrier((sent, theirs[0], *w2_others))
    goals = (kept, lax.ppermute(sent, "grp", CORE))

    teachers = list(zip((w1_dino, w1_sam, w1_siglip), w2s, w2_others))
    firsts = adapt([own], 0, goals, teachers, (0, 1, 2))

    def second(i, to, after=None):
        pieces = list(theirs)
        if after is not None:
            *pieces, after = lax.optimization_barrier((*pieces, after))
        slots = tuple(range(i, to))
        return adapt(pieces, 1, goals, teachers[i:to], slots, firsts[4 * i : 4 * to])

    def gradient(state, after):
        goal, hidden, pred, part = state
        channels = hidden.shape[1]
        scale = channels / math.sqrt(total)
        sums = part + jnp.roll(lax.ppermute(part, "grp", CHIP), own_tokens, axis=1)
        pred_norm = jnp.sqrt(sums[0] + epsilon)
        goal_norm = jnp.sqrt(sums[1] + epsilon)
        product = pred_norm * goal_norm
        on_goal = -scale / product
        on_pred = scale * sums[2] / (product * pred_norm * pred_norm)
        on_goal, on_pred, after = lax.optimization_barrier((on_goal, on_pred, after))
        error = (on_goal[:, None] * goal.astype(f32) + on_pred[:, None] * pred).astype(bf16)
        grad = jnp.einsum("tk,tc->kc", hidden, error, preferred_element_type=f32)
        return grad.astype(bf16)

    dino_state = second(0, 1)
    others = second(1, 3, dino_state[3])
    sam_state, siglip_state = others[:4], others[4:]
    grads = [gradient(dino_state, sam_state[3])]
    grads.append(gradient(sam_state, grads[0]))
    grads.append(gradient(siglip_state, grads[1]))
    received = [lax.ppermute(grad[:, HALF:], "grp", CORE) for grad in grads]
    split = lax.all_to_all(pack(grads, received, n_dp), "dp", 0, 0, tiled=True)
    shapes = [(w.shape[0] // n_dp, w.shape[1]) for w in (w2_dino, w2_siglip, w2_sam)]
    return tuple(unpack(split, shapes))


def solution(mesh):
    in_specs = (
        P("dp", "grp", None, None),
        P("dp", None, None, "grp"),
        P("dp", None, None, "grp"),
        P("dp", None, None, "grp"),
        P(),
        P(None, "grp"),
        P(),
        P(None, "grp"),
        P(),
        P(None, "grp"),
    )
    out_specs = (P("dp", "grp"), P("dp", "grp"), P("dp", "grp"))
    return jax.shard_map(shards, mesh=mesh, in_specs=in_specs, out_specs=out_specs, check_vma=False)
```
